128 devices in a mesh: row: 16 (over y, x), col: 8 (over z, core).
Axes of the slice: x: 4, y: 4, z: 4, core: 2. Of those that a mesh axis runs over, the one named last changes fastest.
Arguments:
- inputs: bfloat16 [1024, 8192], P('col', 'row'), may hold values from -6 to 6
- out_grad: bfloat16 [1024, 8192], P('col', 'row'), may hold values from -1.5 to 1.5
- gate_pre: bfloat16 [1024, 14336], P('row', 'col'), may hold values from -9 to 9
- up_pre: bfloat16 [1024, 14336], P('row', 'col'), may hold values from -6 to 6
- gate_weight: bfloat16 [8192, 14336], P('row', 'col'), may hold values from -0.0625 to 0.0625
- up_weight: bfloat16 [8192, 14336], P('row', 'col'), may hold values from -0.0625 to 0.0625
- down_weight: bfloat16 [14336, 8192], P('col', 'row'), may hold values from -0.046875 to 0.046875
Outputs:
- input_grad: float32 [1024, 8192], P('col', 'row')
- gate_grad: float32 [8192, 14336], P('row', 'col')
- up_grad: float32 [8192, 14336], P('row', 'col')
- down_grad: float32 [14336, 8192], P('col', 'row')
The draws below stay inside these ranges and needn't reach their ends.
All inputs are finite; a program needn't handle non-finite values.
Results may differ from the reference program's by a relative error of at most 0.0029.
Values may be sent and summed in bfloat16 or wider, within the bound.
A program may use at most 128 MiB of HBM per device.

```python
import jax
import jax.numpy as jnp
from jax import lax

D = 8192
FF = 14336
TOKENS = 1024


def strengthened(values, stream_key, source, target, blocks, factor):
    def block_of(dim):
        return (jnp.arange(values.shape[dim]) // (values.shape[dim] // blocks)).reshape((-1,) + (1,) * (values.ndim - 1 - dim))

    one_side = jax.random.permutation(stream_key, blocks)[block_of(target)]
    other_side = (block_of(target) + blocks // 2) % blocks
    return jnp.where((block_of(source) == one_side) | (block_of(source) == other_side), factor * values, values)


def steps_of(key, extent, cuts, least, high):
    level = 1.0
    for axis_at, shards_of in cuts:
        heights = jax.random.uniform(jax.random.fold_in(jax.random.fold_in(key, 6), axis_at), (shards_of,), jnp.float32, least / len(cuts), high / len(cuts))
        level = level * jnp.repeat(jnp.exp(heights), extent[axis_at] // shards_of).reshape((-1,) + (1,) * (len(extent) - 1 - axis_at))
    return level


def normal_values(rng, extent, spread, most, shards=(), kind=jnp.bfloat16):
    drawn = spread * jax.random.normal(rng, extent, jnp.float32)
    if shards:
        drawn = drawn * steps_of(rng, extent, shards, -0.22, 0.18)
    return jnp.clip(drawn, -most, most).astype(kind)


def bell_draw_with(own_key, shape, deviation, reach, shards, heavy, held_as=jnp.bfloat16):
    array = deviation * jax.random.normal(own_key, shape, jnp.float32)
    if shards:
        array = array * steps_of(own_key, shape, shards, -0.22, 0.18)
    return jnp.clip(strengthened(array, jax.random.fold_in(own_key, 3), *heavy), -reach, reach).astype(held_as)


def setup_inputs(seed: int = 0) -> dict:
    streams_of = jax.random.split(jax.random.key(seed), 8)
    inputs = normal_values(streams_of[0], (TOKENS, D), 1.0, 6.0, ((0, 8), (1, 16)))
    out_grad = bell_draw_with(streams_of[1], (TOKENS, D), 0.25, 1.5, ((0, 8), (1, 16)), (1, 0, 16, 2.0))
    gate_pre = normal_values(streams_of[2], (TOKENS, FF), 1.5, 9.0, ((0, 16), (1, 8)))
    up_pre = normal_values(streams_of[3], (TOKENS, FF), 1.0, 6.0, ((0, 16), (1, 8)))
    gate_weight = normal_values(streams_of[4], (D, FF), D ** -0.5, 0.0625, ((0, 16), (1, 8)))
    up_weight = normal_values(streams_of[5], (D, FF), D ** -0.5, 0.0625, ((0, 16), (1, 8)))
    down_weight = normal_values(streams_of[6], (FF, D), FF ** -0.5, 0.046875, ((0, 8), (1, 16)))
    return {"inputs": inputs, "out_grad": out_grad, "gate_pre": gate_pre, "up_pre": up_pre, "gate_weight": gate_weight, "up_weight": up_weight, "down_weight": down_weight}


LEAD_DIMS = (((0,), (0,)), ((), ()))
LAST_DIMS = (((1,), (1,)), ((), ()))


def swiglu_grads(grad_hidden, gate_pre, up_pre):
    gate_val = gate_pre.astype(jnp.float32)
    up_val = up_pre.astype(jnp.float32)
    gate_sig = jax.nn.sigmoid(gate_val)
    hidden = (gate_val * gate_sig * up_val).astype(jnp.bfloat16)
    grad_gate = (grad_hidden * up_val * gate_sig * (1.0 + gate_val * (1.0 - gate_sig))).astype(jnp.bfloat16)
    grad_up = (grad_hidden * gate_val * gate_sig).astype(jnp.bfloat16)
    return hidden, grad_gate, grad_up


def reference(inputs, out_grad, gate_pre, up_pre, gate_weight, up_weight, down_weight):
    grad_hidden = lax.dot_general(out_grad, down_weight, LAST_DIMS, preferred_element_type=jnp.float32)
    hidden, grad_gate, grad_up = swiglu_grads(grad_hidden, gate_pre, up_pre)
    input_grad = lax.dot_general(grad_gate, gate_weight, LAST_DIMS, preferred_element_type=jnp.float32)
    input_grad = input_grad + lax.dot_general(grad_up, up_weight, LAST_DIMS, preferred_element_type=jnp.float32)
    gate_grad = lax.dot_general(inputs, grad_gate, LEAD_DIMS, preferred_element_type=jnp.float32)
    up_grad = lax.dot_general(inputs, grad_up, LEAD_DIMS, preferred_element_type=jnp.float32)
    down_grad = lax.dot_general(hidden, out_grad, LEAD_DIMS, preferred_element_type=jnp.float32)
    return (input_grad, gate_grad, up_grad, down_grad)
```

```python
import jax
import jax.numpy as jnp
from jax import lax
from jax.sharding import PartitionSpec as P

LEAD_DIMS = (((0,), (0,)), ((), ()))
LAST_DIMS = (((1,), (1,)), ((), ()))


def body(inputs, out_grad, gate_pre, up_pre, gate_weight, up_weight, down_weight):
    gate_val = gate_pre.astype(jnp.float32)
    up_val = up_pre.astype(jnp.float32)
    gate_sig = jax.nn.sigmoid(gate_val)
    hidden = (gate_val * gate_sig * up_val).astype(jnp.bfloat16)
    grad_full = lax.all_gather(out_grad, "col", axis=0, tiled=True)
    hidden_all = lax.all_gather(hidden, "row", axis=0, tiled=True)
    partial_sum = lax.dot_general(
        grad_full, down_weight, LAST_DIMS, preferred_element_type=jnp.float32
    )
    grad_hidden = lax.psum_scatter(partial_sum, "row", scatter_dimension=0, tiled=True)
    input_full = lax.all_gather(inputs, "col", axis=0, tiled=True)
    grad_gate = (
        grad_hidden * up_val * gate_sig * (1.0 + gate_val * (1.0 - gate_sig))
    ).astype(jnp.bfloat16)
    grad_up = (grad_hidden * gate_val * gate_sig).astype(jnp.bfloat16)
    down_grad = lax.dot_general(
        hidden_all, grad_full, LEAD_DIMS, preferred_element_type=jnp.float32
    )
    gate_all = lax.all_gather(grad_gate, "row", axis=0, tiled=True)
    up_all = lax.all_gather(grad_up, "row", axis=0, tiled=True)
    total = lax.dot_general(gate_all, gate_weight, LAST_DIMS, preferred_element_type=jnp.float32)
    input_grad = lax.psum_scatter(
        total + lax.dot_general(up_all, up_weight, LAST_DIMS, preferred_element_type=jnp.float32),
        "col",
        scatter_dimension=0,
        tiled=True,
    )
    gate_grad = lax.dot_general(input_full, gate_all, LEAD_DIMS, preferred_element_type=jnp.float32)
    up_grad = lax.dot_general(input_full, up_all, LEAD_DIMS, preferred_element_type=jnp.float32)
    return (input_grad, gate_grad, up_grad, down_grad)


def solution(mesh):
    in_specs = (
        P("col", "row"),
        P("col", "row"),
        P("row", "col"),
        P("row", "col"),
        P("row", "col"),
        P("row", "col"),
        P("col", "row"),
    )
    out_specs = (P("col", "row"), P("row", "col"), P("row", "col"), P("col", "row"))
    return jax.shard_map(body, mesh=mesh, in_specs=in_specs, out_specs=out_specs, check_vma=False)
```

```python
import jax
import jax.numpy as jnp
from jax import lax
from jax.experimental import pallas as pl
from jax.experimental.pallas import tpu as pltpu
from jax.sharding import PartitionSpec as P

MESH = pl.DeviceIdType.MESH
F32 = jnp.float32
BF16 = jnp.bfloat16
NT = (((1,), (1,)), ((), ()))
TN = (((0,), (0,)), ((), ()))
N = 4
ROWS = 16
D = 512
F = 1792
HALF = F // 2
TILE = 256


def _exchange(
    og_ref, in_ref, gate_ref, up_ref, gw_hbm, uw_hbm, dw_hbm,
    ig_ref, all_hbm, in_hbm, og_hbm,
    dw, gw, uw, og_all, in_all, arr, part, sb, ra, vf, rb, ip, ri, rz,
    load_sem, store_sem, og_s, og_r, in_s, in_r, rs_s, rs_r, ag_s, ag_r, ig_s, ig_r,
):
    row, col = lax.axis_index("row"), lax.axis_index("col")
    y, x = row // N, row % N
    z, k = col // 2, col % 2

    def at(base, step):
        return (base + (step + N)) % N

    def chip(axis, step):
        if axis == "y":
            return (at(y, step) * N + x, col)
        return (y * N + at(x, step), col)

    def column(step):
        return (row, (col + step) % 8)

    axes = (("y", "x"), ("x", "y"))
    place = ((y, x), (x, y))
    cols = (pl.ds(0, HALF), pl.ds(HALF, HALF))

    barrier = pltpu.get_barrier_semaphore()
    for axis in ("y", "x"):
        for step in (1, -1):
            pl.semaphore_signal(barrier, inc=1, device_id=chip(axis, step), device_id_type=MESH)
    for step in range(1, 8):
        pl.semaphore_signal(barrier, inc=1, device_id=column(step), device_id_type=MESH)

    loads = [
        pltpu.make_async_copy(dw_hbm, dw, load_sem.at[0]),
        pltpu.make_async_copy(gw_hbm, gw, load_sem.at[1]),
        pltpu.make_async_copy(uw_hbm, uw, load_sem.at[2]),
    ]
    for load in loads:
        load.start()

    for j in range(N):
        for half in range(2):
            own = pl.ds(half * N * ROWS + j * ROWS, ROWS)
            og_all[j, 2 * col + half] = og_ref[own, :]
            in_all[j, 2 * col + half] = in_ref[own, :]

    def remote(src, dst, ssem, rsem, device):
        return pltpu.make_async_remote_copy(
            src_ref=src, dst_ref=dst, send_sem=ssem, recv_sem=rsem,
            device_id=device, device_id_type=MESH,
        )

    def og_copy(j, step, origin):
        block = og_all.at[j, pl.ds(2 * origin, 2)]
        return remote(block, block, og_s.at[j, step - 1], og_r.at[j, step - 1], column(step))

    def in_copy(step, origin):
        block = in_all.at[:, pl.ds(2 * origin, 2)]
        return remote(block, block, in_s.at[step - 1], in_r.at[step - 1], column(step))

    def slots(v):
        return jnp.maximum(2 + 2 * v, 0)

    def item(v):
        return jnp.maximum(1 + v, 0)

    def block(s, first, count, b):
        a = place[s][0]
        if s == 0:
            return arr.at[pl.ds(first, count), a, b, :, cols[s]]
        return arr.at[pl.ds(first, count), b, a, :, cols[s]]

    def group(s, first, count, a):
        if s == 0:
            return arr.at[pl.ds(first, count), a, :, :, cols[s]]
        return arr.at[pl.ds(first, count), :, a, :, cols[s]]

    def ag(kind, v, s, sending):
        a, b = place[s]
        first = slots(v)
        step = 1 if kind % 2 == 0 else -1
        axis = axes[s][1] if kind < 4 else axes[s][0]
        here = b if kind < 4 else a
        if kind in (0, 1, 4, 5):
            lead, count = first, 2
            origin = here if sending else at(here, -step)
        else:
            lead, count = first + (0 if step == 1 else 1), 1
            origin = at(here, -step) if sending else at(here, 2)
        view = block(s, lead, count, origin) if kind < 4 else group(s, lead, count, origin)
        return remote(
            view, view, ag_s.at[kind, item(v), s], ag_r.at[kind, item(v), s], chip(axis, step)
        )

    def ag_a0(v):
        for s in range(2):
            ag(0, v, s, True).start()
            ag(1, v, s, True).start()

    def ag_a1(v):
        for s in range(2):
            for kind in (0, 1):
                ag(kind, v, s, False).wait_recv()
                ag(kind + 2, v, s, True).start()

    def ag_a2(v):
        for s in range(2):
            ag(2, v, s, False).wait_recv()
            ag(3, v, s, False).wait_recv()
            ag(4, v, s, True).start()
            ag(5, v, s, True).start()

    def ag_a3(v):
        for s in range(2):
            for kind in (4, 5):
                ag(kind, v, s, False).wait_recv()
                ag(kind + 2, v, s, True).start()

    def store(v):
        two = pl.ds(slots(v), 2)
        return pltpu.make_async_copy(arr.at[two], all_hbm.at[two], store_sem.at[item(v)])

    def ag_a4(v):
        for s in range(2):
            ag(6, v, s, False).wait_recv()
            ag(7, v, s, False).wait_recv()
        store(v).start()

    def rs(kind, j, s, o, sending):
        step = 1 if o == 0 else -1
        a, b = place[s]
        number = kind % 3
        direction = -step if number == 2 else step
        ssem, rsem = rs_s.at[kind, j, s, o], rs_r.at[kind, j, s, o]
        if kind < 3:
            two = pl.ds(2 * o, 2)
            src = sb.at[number, j, s, two]
            dst = ra.at[number, j, s, two]
            device = chip(axes[s][0], direction)
        else:
            eight = pl.ds(8 * o, 8)
            target = (at(b, 2), at(b, step), at(b, -step))[number]
            src = vf.at[j, s, target, eight]
            dst = rb.at[number, j, s, eight]
            device = chip(axes[s][1], direction)
        return remote(src, dst, ssem, rsem, device)

    def own_part(j, s, a, o):
        two = pl.ds(2 * o, 2)
        if s == 0:
            return part[j, a, two, :, cols[s]]
        return part[j, two, a, :, cols[s]]

    def rs_s0(j):
        for step in range(1, 8):
            og_copy(j, step, (col + 8 - step) % 8).wait_recv()
        lhs = og_all[j].reshape(16 * ROWS, D)

        @pl.loop(0, F // TILE)
        def _(n):
            at_n = pl.ds(pl.multiple_of(n * TILE, TILE), TILE)
            out = lax.dot_general(lhs, dw[at_n, :], NT, preferred_element_type=F32)
            part[j, :, :, :, at_n] = out.reshape(N, N, ROWS, TILE)

        for s in range(2):
            a = place[s][0]
            for o in range(2):
                step = 1 if o == 0 else -1
                two = pl.ds(2 * o, 2)
                sb[0, j, s, two] = own_part(j, s, at(a, 2), o).astype(BF16)
                rs(0, j, s, o, True).start()
        for s in range(2):
            a = place[s][0]
            for o in range(2):
                step = 1 if o == 0 else -1
                two = pl.ds(2 * o, 2)
                sb[2, j, s, two] = own_part(j, s, at(a, -step), o).astype(BF16)
                rs(2, j, s, o, True).start()

    def rs_s1(j):
        for s in range(2):
            a = place[s][0]
            for o in range(2):
                step = 1 if o == 0 else -1
                two = pl.ds(2 * o, 2)
                rs(0, j, s, o, False).wait_recv()
                total = own_part(j, s, at(a, step), o) + ra[0, j, s, two].astype(F32)
                sb[1, j, s, two] = total.astype(BF16)
                rs(1, j, s, o, True).start()

    def rs_s2(j):
        for s in range(2):
            a = place[s][0]
            for o in range(2):
                two = pl.ds(2 * o, 2)
                rs(2, j, s, o, False).wait_recv()
                rs(1, j, s, o, False).wait_recv()
                vf[j, s, two] = (
                    own_part(j, s, a, o)
                    + ra[1, j, s, two].astype(F32)
                    + ra[2, j, s, two].astype(F32)
                )
            for o in range(2):
                rs(3, j, s, o, True).start()
                rs(5, j, s, o, True).start()

    def rs_s3(j):
        for s in range(2):
            b = place[s][1]
            for o in range(2):
                step = 1 if o == 0 else -1
                eight = pl.ds(8 * o, 8)
                rs(3, j, s, o, False).wait_recv()
                vf[j, s, at(b, step), eight] = vf[j, s, at(b, step), eight] + rb[0, j, s, eight]
                rs(4, j, s, o, True).start()

    def pre(j, s):
        own = pl.ds(pl.multiple_of(j * ROWS, ROWS), ROWS)
        gate = gate_ref[own, cols[s]].astype(F32)
        up = up_ref[own, cols[s]].astype(F32)
        return gate, up, 1.0 / (1.0 + jnp.exp(-gate))

    def rs_s4(j):
        for s in range(2):
            b = place[s][1]
            for o in range(2):
                rs(5, j, s, o, False).wait_recv()
                rs(4, j, s, o, False).wait_recv()
            grad = vf[j, s, b] + rb[1, j, s] + rb[2, j, s]
            gate, up, sig = pre(j, s)
            first = slots(j)
            arr[first, y, x, :, cols[s]] = (grad * up * sig * (1.0 + gate * (1.0 - sig))).astype(BF16)
            arr[first + 1, y, x, :, cols[s]] = (grad * gate * sig).astype(BF16)
            ag(0, j, s, True).start()
            ag(1, j, s, True).start()

    def hidden(slot, j):
        for s in range(2):
            gate, up, sig = pre(j, s)
            arr[slot, y, x, :, cols[s]] = (gate * sig * up).astype(BF16)

    def ig_pair(j):
        return remote(ip.at[j, :, 1 - k], ri.at[j], ig_s.at[0, j], ig_r.at[0, j], (row, 2 * z + 1 - k))

    def ig_send(j, step):
        return remote(
            ip.at[j, at(z, step), k], rz.at[j, step - 1],
            ig_s.at[step, j], ig_r.at[step, j], (row, 2 * at(z, step) + k),
        )

    def ig_i0(j):
        first = slots(j)
        for n in range(D // TILE):
            at_n = pl.ds(n * TILE, TILE)
            out = lax.dot_general(
                arr[first].reshape(16 * ROWS, F), gw[at_n, :], NT, preferred_element_type=F32
            ) + lax.dot_general(
                arr[first + 1].reshape(16 * ROWS, F), uw[at_n, :], NT, preferred_element_type=F32
            )
            ip[j, :, :, :, :, at_n] = out.reshape(N, 2, 2, ROWS, TILE)
        ig_pair(j).start()

    def ig_i1(j):
        ig_pair(j).wait_recv()
        for step in (2, 1, 3, 0):
            t = at(z, step)
            ip[j, t, k] = ip[j, t, k] + ri[j, t]
            if step:
                ig_send(j, step).start()

    def ig_i2(j):
        for step in (1, 2, 3):
            ig_send(j, step).wait_recv()
        total = ip[j, z, k] + rz[j, 0] + rz[j, 1] + rz[j, 2]
        for half in range(2):
            own = pl.ds(pl.multiple_of(half * N * ROWS + j * ROWS, ROWS), ROWS)
            ig_ref[own, :] = total[half]

    pl.semaphore_wait(barrier, 11)
    for j in range(N):
        for step in (4, 3, 5, 2, 6, 1, 7):
            og_copy(j, step, col).start()
    hidden(0, 0)
    hidden(1, 1)
    ag_a0(-6)
    for step in (4, 3, 5, 2, 6, 1, 7):
        in_copy(step, col).start()
    hidden(10, 2)
    hidden(11, 3)
    ag_a0(4)
    ag_a1(-6)
    ag_a2(-6)
    loads[0].wait()

    def stage(t, number, count, call):
        j = t - number

        @pl.when((j >= 0) & (j < count))
        def _():
            call(j)

    @pl.loop(0, 14)
    def _(t):
        stage(t, 4, N, rs_s4)
        stage(t, 3, N, rs_s3)
        stage(t, 2, N, rs_s2)
        stage(t, 1, N, rs_s1)
        stage(t, 0, N, rs_s0)

        @pl.when(t == 1)
        def _():
            ag_a3(-6)

        @pl.when(t == 7)
        def _():
            loads[1].wait()
            loads[2].wait()

        stage(t, 5, N + 1, ag_a1)
        stage(t, 6, N + 1, ag_a2)
        stage(t, 7, N + 1, ag_a3)
        stage(t, 9, N, ig_i1)
        stage(t, 8, N, ag_a4)
        stage(t, 8, N, ig_i0)
        stage(t, 10, N, ig_i2)

        @pl.when(t == 6)
        def _():
            ag_a4(-6)

        @pl.when(t == 9)
        def _():
            for step in range(1, 8):
                in_copy(step, (col + 8 - step) % 8).wait_recv()
            pltpu.make_async_copy(in_all, in_hbm, store_sem.at[6]).start()
            pltpu.make_async_copy(og_all, og_hbm, store_sem.at[7]).start()

    ag_a4(4)
    for j in range(N):
        for step in range(1, 8):
            og_copy(j, step, col).wait_send()
    for step in range(1, 8):
        in_copy(step, col).wait_send()

    @pl.loop(0, N)
    def _(j):
        for s in range(2):
            for o in range(2):
                for kind in range(6):
                    rs(kind, j, s, o, True).wait_send()
        ig_pair(j).wait_send()
        for step in (1, 2, 3):
            ig_send(j, step).wait_send()

    @pl.loop(0, 6)
    def _(i):
        for s in range(2):
            for kind in range(8):
                ag(kind, i - 1, s, True).wait_send()
        store(i - 1).wait()

    pltpu.make_async_copy(in_all, in_hbm, store_sem.at[6]).wait()
    pltpu.make_async_copy(og_all, og_hbm, store_sem.at[7]).wait()


def exchange(out_grad, inputs, gate_pre, up_pre, gate_weight, up_weight, down_weight):
    vmem = pl.BlockSpec(memory_space=pltpu.VMEM)
    hbm = pl.BlockSpec(memory_space=pl.ANY)
    dma = pltpu.SemaphoreType.DMA
    return pl.pallas_call(
        _exchange,
        out_shape=(
            jax.ShapeDtypeStruct((128, D), F32),
            jax.ShapeDtypeStruct((12, N, N, ROWS, F), BF16),
            jax.ShapeDtypeStruct((N, 16, ROWS, D), BF16),
            jax.ShapeDtypeStruct((N, 16, ROWS, D), BF16),
        ),
        in_specs=[vmem] * 4 + [hbm] * 3,
        out_specs=(vmem, hbm, hbm, hbm),
        scratch_shapes=[
            pltpu.VMEM((F, D), BF16),
            pltpu.VMEM((D, F), BF16),
            pltpu.VMEM((D, F), BF16),
            pltpu.VMEM((N, 16, ROWS, D), BF16),
            pltpu.VMEM((N, 16, ROWS, D), BF16),
            pltpu.VMEM((12, N, N, ROWS, F), BF16),
            pltpu.VMEM((N, N, N, ROWS, F), F32),
            pltpu.VMEM((3, N, 2, N, ROWS, HALF), BF16),
            pltpu.VMEM((3, N, 2, N, ROWS, HALF), BF16),
            pltpu.VMEM((N, 2, N, ROWS, HALF), F32),
            pltpu.VMEM((3, N, 2, ROWS, HALF), F32),
            pltpu.VMEM((N, N, 2, 2, ROWS, D), F32),
            pltpu.VMEM((N, N, 2, ROWS, D), F32),
            pltpu.VMEM((N, 3, 2, ROWS, D), F32),
            dma((3,)),
            dma((8,)),
            dma((N, 7)),
            dma((N, 7)),
            dma((7,)),
            dma((7,)),
            dma((6, N, 2, 2)),
            dma((6, N, 2, 2)),
            dma((8, 6, 2)),
            dma((8, 6, 2)),
            dma((4, N)),
            dma((4, N)),
        ],
        compiler_params=pltpu.CompilerParams(
            collective_id=0, has_side_effects=True, vmem_limit_bytes=58 << 20
        ),
        cost_estimate=pl.CostEstimate(
            flops=6 * 1024 * D * F, bytes_accessed=20 << 20, transcendentals=64 * F
        ),
        name="exchange",
    )(out_grad, inputs, gate_pre, up_pre, gate_weight, up_weight, down_weight)


def _weights(arr_ref, in_ref, og_ref, gg_ref, ug_ref, dg_ref):
    def tokens(numbers):
        return jnp.concatenate([arr_ref[n] for n in numbers], axis=0)

    inputs, out_grad = in_ref[...], og_ref[...]
    gg_ref[...] = lax.dot_general(inputs, tokens((2, 4, 6, 8)), TN, preferred_element_type=F32)
    ug_ref[...] = lax.dot_general(inputs, tokens((3, 5, 7, 9)), TN, preferred_element_type=F32)
    dg_ref[...] = lax.dot_general(tokens((0, 1, 10, 11)), out_grad, TN, preferred_element_type=F32)


def weights(arr, inputs, out_grad):
    return pl.pallas_call(
        _weights,
        grid=(F // TILE,),
        out_shape=(
            jax.ShapeDtypeStruct((D, F), F32),
            jax.ShapeDtypeStruct((D, F), F32),
            jax.ShapeDtypeStruct((F, D), F32),
        ),
        in_specs=[
            pl.BlockSpec((12, 256, TILE), lambda n: (0, 0, n)),
            pl.BlockSpec((1024, D), lambda n: (0, 0)),
            pl.BlockSpec((1024, D), lambda n: (0, 0)),
        ],
        out_specs=(
            pl.BlockSpec((D, TILE), lambda n: (0, n)),
            pl.BlockSpec((D, TILE), lambda n: (0, n)),
            pl.BlockSpec((TILE, D), lambda n: (n, 0)),
        ),
        compiler_params=pltpu.CompilerParams(vmem_limit_bytes=40 << 20),
        name="weights",
    )(arr, inputs, out_grad)


def body(inputs, out_grad, gate_pre, up_pre, gate_weight, up_weight, down_weight):
    input_grad, arr, in_all, og_all = exchange(
        out_grad, inputs, gate_pre, up_pre, gate_weight, up_weight, down_weight
    )
    gate_grad, up_grad, down_grad = weights(
        arr.reshape(12, 256, F), in_all.reshape(1024, D), og_all.reshape(1024, D)
    )
    return (input_grad, gate_grad, up_grad, down_grad)


def solution(mesh):
    in_specs = (
        P("col", "row"),
        P("col", "row"),
        P("row", "col"),
        P("row", "col"),
        P("row", "col"),
        P("row", "col"),
        P("col", "row"),
    )
    out_specs = (P("col", "row"), P("row", "col"), P("row", "col"), P("col", "row"))
    return jax.shard_map(body, mesh=mesh, in_specs=in_specs, out_specs=out_specs, check_vma=False)
```

```python
import jax
import jax.numpy as jnp
from jax import lax
from jax.experimental import pallas as pl
from jax.experimental.pallas import tpu as pltpu
from jax.sharding import PartitionSpec as P

MESH = pl.DeviceIdType.MESH
F32 = jnp.float32
BF16 = jnp.bfloat16
NT = (((1,), (1,)), ((), ()))
TN = (((0,), (0,)), ((), ()))
N = 4
ROWS = 16
D = 512
F = 1792
HALF = F // 2
TILE = 256


def _exchange(
    og_ref, in_ref, gate_ref, up_ref, gw_hbm, uw_hbm, dw_hbm,
    ig_ref, gg_ref, ug_ref, dg_ref,
    dw, gw, uw, og_all, in_all, in_t, arr, part, sb, ra, vf, rb, ip, ri, rz,
    load_sem, og_s, og_r, in_s, in_r, rs_s, rs_r, ag_s, ag_r, ig_s, ig_r,
):
    row, col = lax.axis_index("row"), lax.axis_index("col")
    y, x = row // N, row % N
    z, k = col // 2, col % 2

    def at(base, step):
        return (base + (step + N)) % N

    def chip(axis, step):
        if axis == "y":
            return (at(y, step) * N + x, col)
        return (y * N + at(x, step), col)

    def column(step):
        return (row, (col + step) % 8)

    axes = (("y", "x"), ("x", "y"))
    place = ((y, x), (x, y))
    cols = (pl.ds(0, HALF), pl.ds(HALF, HALF))

    barrier = pltpu.get_barrier_semaphore()
    for axis in ("y", "x"):
        for step in (1, -1):
            pl.semaphore_signal(barrier, inc=1, device_id=chip(axis, step), device_id_type=MESH)
    for step in range(1, 8):
        pl.semaphore_signal(barrier, inc=1, device_id=column(step), device_id_type=MESH)

    loads = [
        pltpu.make_async_copy(dw_hbm, dw, load_sem.at[0]),
        pltpu.make_async_copy(gw_hbm, gw, load_sem.at[1]),
        pltpu.make_async_copy(uw_hbm, uw, load_sem.at[2]),
    ]
    for load in loads:
        load.start()

    for j in range(N):
        for half in range(2):
            own = pl.ds(half * N * ROWS + j * ROWS, ROWS)
            og_all[j, 2 * col + half] = og_ref[own, :]
            in_all[j, 2 * col + half] = in_ref[own, :]

    def remote(src, dst, ssem, rsem, device):
        return pltpu.make_async_remote_copy(
            src_ref=src, dst_ref=dst, send_sem=ssem, recv_sem=rsem,
            device_id=device, device_id_type=MESH,
        )

    def og_copy(j, step, origin):
        block = og_all.at[j, pl.ds(2 * origin, 2)]
        return remote(block, block, og_s.at[j, step - 1], og_r.at[j, step - 1], column(step))

    def in_copy(step, origin):
        block = in_all.at[:, pl.ds(2 * origin, 2)]
        return remote(block, block, in_s.at[step - 1], in_r.at[step - 1], column(step))

    def slots(v):
        return jnp.clip(2 + 2 * v, 0, 10)

    def item(v):
        return jnp.clip(1 + v, 0, 5)

    def block(s, first, count, b):
        a = place[s][0]
        if s == 0:
            return arr.at[pl.ds(first, count), a, b, :, cols[s]]
        return arr.at[pl.ds(first, count), b, a, :, cols[s]]

    def group(s, first, count, a):
        if s == 0:
            return arr.at[pl.ds(first, count), a, :, :, cols[s]]
        return arr.at[pl.ds(first, count), :, a, :, cols[s]]

    def ag(kind, v, s, sending):
        a, b = place[s]
        first = slots(v)
        step = 1 if kind % 2 == 0 else -1
        axis = axes[s][1] if kind < 4 else axes[s][0]
        here = b if kind < 4 else a
        if kind in (0, 1, 4, 5):
            lead, count = first, 2
            origin = here if sending else at(here, -step)
        else:
            lead, count = first + (0 if step == 1 else 1), 1
            origin = at(here, -step) if sending else at(here, 2)
        view = block(s, lead, count, origin) if kind < 4 else group(s, lead, count, origin)
        return remote(
            view, view, ag_s.at[kind, item(v), s], ag_r.at[kind, item(v), s], chip(axis, step)
        )

    def ag_a0(v):
        for s in range(2):
            ag(0, v, s, True).start()
            ag(1, v, s, True).start()

    def ag_a1(v):
        for s in range(2):
            for kind in (0, 1):
                ag(kind, v, s, False).wait_recv()
                ag(kind + 2, v, s, True).start()

    def ag_a2(v):
        for s in range(2):
            ag(2, v, s, False).wait_recv()
            ag(3, v, s, False).wait_recv()
            ag(4, v, s, True).start()
            ag(5, v, s, True).start()

    def ag_a3(v):
        for s in range(2):
            for kind in (4, 5):
                ag(kind, v, s, False).wait_recv()
                ag(kind + 2, v, s, True).start()

    def ag_a4(v):
        for s in range(2):
            ag(6, v, s, False).wait_recv()
            ag(7, v, s, False).wait_recv()

    def rs(kind, j, s, o, sending):
        step = 1 if o == 0 else -1
        a, b = place[s]
        number = kind % 3
        direction = -step if number == 2 else step
        ssem, rsem = rs_s.at[kind, j, s, o], rs_r.at[kind, j, s, o]
        if kind < 3:
            two = pl.ds(2 * o, 2)
            src = sb.at[number, j, s, two]
            dst = ra.at[number, j, s, two]
            device = chip(axes[s][0], direction)
        else:
            eight = pl.ds(8 * o, 8)
            target = (at(b, 2), at(b, step), at(b, -step))[number]
            src = vf.at[j, s, target, eight]
            dst = rb.at[number, j, s, eight]
            device = chip(axes[s][1], direction)
        return remote(src, dst, ssem, rsem, device)

    def own_part(j, s, a, o):
        two = pl.ds(2 * o, 2)
        if s == 0:
            return part[j, a, two, :, cols[s]]
        return part[j, two, a, :, cols[s]]

    def rs_s0(j):
        for step in range(1, 8):
            og_copy(j, step, (col + 8 - step) % 8).wait_recv()
        lhs = og_all[j].reshape(16 * ROWS, D)

        @pl.loop(0, F // TILE)
        def _(n):
            at_n = pl.ds(pl.multiple_of(n * TILE, TILE), TILE)
            out = lax.dot_general(lhs, dw[at_n, :], NT, preferred_element_type=F32)
            part[j, :, :, :, at_n] = out.reshape(N, N, ROWS, TILE)

        for s in range(2):
            a = place[s][0]
            for o in range(2):
                step = 1 if o == 0 else -1
                two = pl.ds(2 * o, 2)
                sb[0, j, s, two] = own_part(j, s, at(a, 2), o).astype(BF16)
                rs(0, j, s, o, True).start()
        for s in range(2):
            a = place[s][0]
            for o in range(2):
                step = 1 if o == 0 else -1
                two = pl.ds(2 * o, 2)
                sb[2, j, s, two] = own_part(j, s, at(a, -step), o).astype(BF16)
                rs(2, j, s, o, True).start()

    def rs_s1(j):
        for s in range(2):
            a = place[s][0]
            for o in range(2):
                step = 1 if o == 0 else -1
                two = pl.ds(2 * o, 2)
                rs(0, j, s, o, False).wait_recv()
                total = own_part(j, s, at(a, step), o) + ra[0, j, s, two].astype(F32)
                sb[1, j, s, two] = total.astype(BF16)
                rs(1, j, s, o, True).start()

    def rs_s2(j):
        for s in range(2):
            a = place[s][0]
            for o in range(2):
                two = pl.ds(2 * o, 2)
                rs(2, j, s, o, False).wait_recv()
                rs(1, j, s, o, False).wait_recv()
                vf[j, s, two] = (
                    own_part(j, s, a, o)
                    + ra[1, j, s, two].astype(F32)
                    + ra[2, j, s, two].astype(F32)
                )
            for o in range(2):
                rs(3, j, s, o, True).start()
                rs(5, j, s, o, True).start()

    def rs_s3(j):
        for s in range(2):
            b = place[s][1]
            for o in range(2):
                step = 1 if o == 0 else -1
                eight = pl.ds(8 * o, 8)
                rs(3, j, s, o, False).wait_recv()
                vf[j, s, at(b, step), eight] = vf[j, s, at(b, step), eight] + rb[0, j, s, eight]
                rs(4, j, s, o, True).start()

    def pre(j, s):
        own = pl.ds(pl.multiple_of(j * ROWS, ROWS), ROWS)
        gate = gate_ref[own, cols[s]].astype(F32)
        up = up_ref[own, cols[s]].astype(F32)
        return gate, up, 1.0 / (1.0 + jnp.exp(-gate))

    def rs_s4(j):
        for s in range(2):
            b = place[s][1]
            for o in range(2):
                rs(5, j, s, o, False).wait_recv()
                rs(4, j, s, o, False).wait_recv()
            grad = vf[j, s, b] + rb[1, j, s] + rb[2, j, s]
            gate, up, sig = pre(j, s)
            first = slots(j)
            arr[first, y, x, :, cols[s]] = (grad * up * sig * (1.0 + gate * (1.0 - sig))).astype(BF16)
            arr[first + 1, y, x, :, cols[s]] = (grad * gate * sig).astype(BF16)
            ag(0, j, s, True).start()
            ag(1, j, s, True).start()

    def hidden(slot, j):
        for s in range(2):
            gate, up, sig = pre(j, s)
            arr[slot, y, x, :, cols[s]] = (gate * sig * up).astype(BF16)

    def ig_pair(j):
        return remote(ip.at[j, :, 1 - k], ri.at[j], ig_s.at[0, j], ig_r.at[0, j], (row, 2 * z + 1 - k))

    def ig_send(j, step):
        return remote(
            ip.at[j, at(z, step), k], rz.at[j, step - 1],
            ig_s.at[step, j], ig_r.at[step, j], (row, 2 * at(z, step) + k),
        )

    def ig_i0(j):
        first = slots(j)
        for n in range(D // TILE):
            at_n = pl.ds(n * TILE, TILE)
            out = lax.dot_general(
                arr[first].reshape(16 * ROWS, F), gw[at_n, :], NT, preferred_element_type=F32
            ) + lax.dot_general(
                arr[first + 1].reshape(16 * ROWS, F), uw[at_n, :], NT, preferred_element_type=F32
            )
            ip[j, :, :, :, :, at_n] = out.reshape(N, 2, 2, ROWS, TILE)
        ig_pair(j).start()

    def ig_i1(j):
        ig_pair(j).wait_recv()
        for step in (2, 1, 3, 0):
            t = at(z, step)
            ip[j, t, k] = ip[j, t, k] + ri[j, t]
            if step:
                ig_send(j, step).start()

    def ig_i2(j):
        for step in (1, 2, 3):
            ig_send(j, step).wait_recv()
        total = ip[j, z, k] + rz[j, 0] + rz[j, 1] + rz[j, 2]
        for half in range(2):
            own = pl.ds(pl.multiple_of(half * N * ROWS + j * ROWS, ROWS), ROWS)
            ig_ref[own, :] = total[half]

    def wg(j):
        first = slots(j)
        for ref, slot in ((gg_ref, first), (ug_ref, first + 1)):

            @pl.loop(0, F // TILE)
            def _(n):
                at_n = pl.ds(pl.multiple_of(n * TILE, TILE), TILE)
                rhs = arr[slot, :, :, :, at_n].reshape(16 * ROWS, TILE)
                out = jnp.dot(in_t[j], rhs, preferred_element_type=F32)

                @pl.when(j == 0)
                def _():
                    ref[:, at_n] = out

                @pl.when(j > 0)
                def _():
                    ref[:, at_n] = ref[:, at_n] + out

    def dg(slot, j, fresh):
        @pl.loop(0, F // TILE)
        def _(n):
            at_n = pl.ds(pl.multiple_of(n * TILE, TILE), TILE)
            out = ref_dot(slot, j, at_n) + ref_dot(slot + 1, j + 1, at_n)
            dg_ref[at_n, :] = out if fresh else dg_ref[at_n, :] + out

    def ref_dot(slot, j, at_n):
        lhs = arr[slot, :, :, :, at_n].reshape(16 * ROWS, TILE)
        rhs = og_all[j].reshape(16 * ROWS, D)
        return lax.dot_general(lhs, rhs, TN, preferred_element_type=F32)

    pl.semaphore_wait(barrier, 11)
    for j in range(N):
        for step in (4, 3, 5, 2, 6, 1, 7):
            og_copy(j, step, col).start()
    hidden(0, 0)
    hidden(1, 1)
    ag_a0(-6)
    for step in (4, 3, 5, 2, 6, 1, 7):
        in_copy(step, col).start()
    hidden(10, 2)
    hidden(11, 3)
    ag_a0(4)
    ag_a1(-6)
    ag_a2(-6)
    loads[0].wait()

    def stage(t, number, count, call):
        j = t - number

        @pl.when((j >= 0) & (j < count))
        def _():
            call(j)

    def ag_stage(t, number, call):
        v = t - number

        @pl.when(((v >= 0) & (v < N)) | (v == N + 1))
        def _():
            call(v)

    @pl.loop(0, 14)
    def _(t):
        stage(t, 4, N, rs_s4)
        stage(t, 3, N, rs_s3)
        stage(t, 2, N, rs_s2)
        stage(t, 1, N, rs_s1)
        stage(t, 0, N, rs_s0)

        @pl.when(t == 1)
        def _():
            ag_a3(-6)

        @pl.when(t == 7)
        def _():
            loads[1].wait()
            loads[2].wait()

        ag_stage(t, 5, ag_a1)
        ag_stage(t, 6, ag_a2)
        ag_stage(t, 7, ag_a3)
        stage(t, 9, N, ig_i1)
        stage(t, 9, N, wg)
        stage(t, 8, N, ag_a4)
        stage(t, 8, N, ig_i0)
        stage(t, 10, N, ig_i2)

        @pl.when(t == 6)
        def _():
            ag_a4(-6)
            dg(0, 0, True)

        @pl.when(t == 7)
        def _():
            for step in range(1, 8):
                in_copy(step, (col + 8 - step) % 8).wait_recv()
            for j in range(N):
                in_t[j] = in_all[j].reshape(16 * ROWS, D).T

    ag_a4(4)
    dg(10, 2, False)
    for j in range(N):
        for step in range(1, 8):
            og_copy(j, step, col).wait_send()
    for step in range(1, 8):
        in_copy(step, col).wait_send()

    @pl.loop(0, N)
    def _(j):
        for s in range(2):
            for o in range(2):
                for kind in range(6):
                    rs(kind, j, s, o, True).wait_send()
        ig_pair(j).wait_send()
        for step in (1, 2, 3):
            ig_send(j, step).wait_send()

    @pl.loop(0, 6)
    def _(i):
        for s in range(2):
            for kind in range(8):
                ag(kind, i - 1, s, True).wait_send()


def exchange(out_grad, inputs, gate_pre, up_pre, gate_weight, up_weight, down_weight):
    vmem = pl.BlockSpec(memory_space=pltpu.VMEM)
    hbm = pl.BlockSpec(memory_space=pl.ANY)
    dma = pltpu.SemaphoreType.DMA
    return pl.pallas_call(
        _exchange,
        out_shape=(
            pltpu.VMEM((128, D), F32),
            pltpu.VMEM((D, F), F32),
            pltpu.VMEM((D, F), F32),
            pltpu.VMEM((F, D), F32),
        ),
        in_specs=[vmem] * 4 + [hbm] * 3,
        out_specs=(vmem, vmem, vmem, vmem),
        scratch_shapes=[
            pltpu.VMEM((F, D), BF16),
            pltpu.VMEM((D, F), BF16),
            pltpu.VMEM((D, F), BF16),
            pltpu.VMEM((N, 16, ROWS, D), BF16),
            pltpu.VMEM((N, 16, ROWS, D), BF16),
            pltpu.VMEM((N, D, 16 * ROWS), BF16),
            pltpu.VMEM((12, N, N, ROWS, F), BF16),
            pltpu.VMEM((N, N, N, ROWS, F), F32),
            pltpu.VMEM((3, N, 2, N, ROWS, HALF), BF16),
            pltpu.VMEM((3, N, 2, N, ROWS, HALF), BF16),
            pltpu.VMEM((N, 2, N, ROWS, HALF), F32),
            pltpu.VMEM((3, N, 2, ROWS, HALF), F32),
            pltpu.VMEM((N, N, 2, 2, ROWS, D), F32),
            pltpu.VMEM((N, N, 2, ROWS, D), F32),
            pltpu.VMEM((N, 3, 2, ROWS, D), F32),
            dma((3,)),
            dma((N, 7)),
            dma((N, 7)),
            dma((7,)),
            dma((7,)),
            dma((6, N, 2, 2)),
            dma((6, N, 2, 2)),
            dma((8, 6, 2)),
            dma((8, 6, 2)),
            dma((4, N)),
            dma((4, N)),
        ],
        compiler_params=pltpu.CompilerParams(
            collective_id=0, has_side_effects=True, vmem_limit_bytes=51 << 20
        ),
        cost_estimate=pl.CostEstimate(
            flops=6 * 1024 * D * F, bytes_accessed=20 << 20, transcendentals=64 * F
        ),
        name="exchange",
    )(out_grad, inputs, gate_pre, up_pre, gate_weight, up_weight, down_weight)


def _write(a, b, c, d, a_out, b_out, c_out, d_out, sem):
    copies = []
    for i, (src, dst) in enumerate(((b, b_out), (c, c_out), (d, d_out), (a, a_out))):
        copies.append(pltpu.make_async_copy(src, dst, sem.at[i]))
        copies[i].start()
    for copy in copies:
        copy.wait()


def write(*grads):
    grads = [pltpu.with_memory_space_constraint(g, pltpu.VMEM) for g in grads]
    hbm = pl.BlockSpec(memory_space=pl.ANY)
    return pl.pallas_call(
        _write,
        out_shape=[pltpu.HBM(g.shape, g.dtype) for g in grads],
        in_specs=[pl.BlockSpec(memory_space=pltpu.VMEM)] * 4,
        out_specs=[hbm] * 4,
        scratch_shapes=[pltpu.SemaphoreType.DMA((4,))],
        compiler_params=pltpu.CompilerParams(vmem_limit_bytes=2 << 20),
        name="write",
    )(*grads)


def body(inputs, out_grad, gate_pre, up_pre, gate_weight, up_weight, down_weight):
    grads = exchange(out_grad, inputs, gate_pre, up_pre, gate_weight, up_weight, down_weight)
    return tuple(write(*grads))


def solution(mesh):
    in_specs = (
        P("col", "row"),
        P("col", "row"),
        P("row", "col"),
        P("row", "col"),
        P("row", "col"),
        P("row", "col"),
        P("col", "row"),
    )
    out_specs = (P("col", "row"), P("row", "col"), P("row", "col"), P("col", "row"))
    return jax.shard_map(body, mesh=mesh, in_specs=in_specs, out_specs=out_specs, check_vma=False)
```

```python
import jax
import jax.numpy as jnp
from jax import lax
from jax.experimental import pallas as pl
from jax.experimental.pallas import tpu as pltpu
from jax.sharding import PartitionSpec as P

MESH = pl.DeviceIdType.MESH
F32 = jnp.float32
BF16 = jnp.bfloat16
NT = (((1,), (1,)), ((), ()))
TN = (((0,), (0,)), ((), ()))
N = 4
ROWS = 16
D = 512
F = 1792
HALF = F // 2
TILE = 256


def _exchange(
    og_hbm, in_hbm, gate_hbm, up_hbm, gw_hbm, uw_hbm, dw_hbm,
    ig_ref, gg_ref, ug_ref, arr, og_all,
    og_ref, in_ref, gate_ref, up_ref, dw, gw, uw, in_all, in_t, part, sb, ra, vf, rb, ip, ri, rz,
    load_sem, og_s, og_r, in_s, in_r, rs_s, rs_r, ag_s, ag_r, ig_s, ig_r,
):
    row, col = lax.axis_index("row"), lax.axis_index("col")
    y, x = row // N, row % N
    z, k = col // 2, col % 2

    def at(base, step):
        return (base + (step + N)) % N

    def chip(axis, step):
        if axis == "y":
            return (at(y, step) * N + x, col)
        return (y * N + at(x, step), col)

    def column(step):
        return (row, (col + step) % 8)

    axes = (("y", "x"), ("x", "y"))
    place = ((y, x), (x, y))
    cols = (pl.ds(0, HALF), pl.ds(HALF, HALF))

    barrier = pltpu.get_barrier_semaphore()
    for axis in ("y", "x"):
        for step in (1, -1):
            pl.semaphore_signal(barrier, inc=1, device_id=chip(axis, step), device_id_type=MESH)
    for step in range(1, 8):
        pl.semaphore_signal(barrier, inc=1, device_id=column(step), device_id_type=MESH)

    loads = [
        pltpu.make_async_copy(og_hbm, og_ref, load_sem.at[3]),
        pltpu.make_async_copy(in_hbm, in_ref, load_sem.at[4]),
        pltpu.make_async_copy(gate_hbm, gate_ref, load_sem.at[5]),
        pltpu.make_async_copy(up_hbm, up_ref, load_sem.at[6]),
        pltpu.make_async_copy(dw_hbm, dw, load_sem.at[0]),
        pltpu.make_async_copy(gw_hbm, gw, load_sem.at[1]),
        pltpu.make_async_copy(uw_hbm, uw, load_sem.at[2]),
    ]
    for load in loads:
        load.start()

    loads[0].wait()
    loads[1].wait()
    for j in range(N):
        for half in range(2):
            own = pl.ds(half * N * ROWS + j * ROWS, ROWS)
            og_all[j, 2 * col + half] = og_ref[own, :]
            in_all[j, 2 * col + half] = in_ref[own, :]

    def remote(src, dst, ssem, rsem, device):
        return pltpu.make_async_remote_copy(
            src_ref=src, dst_ref=dst, send_sem=ssem, recv_sem=rsem,
            device_id=device, device_id_type=MESH,
        )

    def og_copy(j, step, origin):
        block = og_all.at[j, pl.ds(2 * origin, 2)]
        return remote(block, block, og_s.at[j, step - 1], og_r.at[j, step - 1], column(step))

    def in_copy(step, origin):
        block = in_all.at[:, pl.ds(2 * origin, 2)]
        return remote(block, block, in_s.at[step - 1], in_r.at[step - 1], column(step))

    def slots(v):
        return jnp.clip(2 + 2 * v, 0, 10)

    def item(v):
        return jnp.clip(1 + v, 0, 5)

    def block(s, first, count, b):
        a = place[s][0]
        if s == 0:
            return arr.at[pl.ds(first, count), a, b, :, cols[s]]
        return arr.at[pl.ds(first, count), b, a, :, cols[s]]

    def group(s, first, count, a):
        if s == 0:
            return arr.at[pl.ds(first, count), a, :, :, cols[s]]
        return arr.at[pl.ds(first, count), :, a, :, cols[s]]

    def ag(kind, v, s, sending):
        a, b = place[s]
        first = slots(v)
        step = 1 if kind % 2 == 0 else -1
        axis = axes[s][1] if kind < 4 else axes[s][0]
        here = b if kind < 4 else a
        if kind in (0, 1, 4, 5):
            lead, count = first, 2
            origin = here if sending else at(here, -step)
        else:
            lead, count = first + (0 if step == 1 else 1), 1
            origin = at(here, -step) if sending else at(here, 2)
        view = block(s, lead, count, origin) if kind < 4 else group(s, lead, count, origin)
        return remote(
            view, view, ag_s.at[kind, item(v), s], ag_r.at[kind, item(v), s], chip(axis, step)
        )

    def ag_a0(v):
        for s in range(2):
            ag(0, v, s, True).start()
            ag(1, v, s, True).start()

    def ag_a1(v):
        for s in range(2):
            for kind in (0, 1):
                ag(kind, v, s, False).wait_recv()
                ag(kind + 2, v, s, True).start()

    def ag_a2(v):
        for s in range(2):
            ag(2, v, s, False).wait_recv()
            ag(3, v, s, False).wait_recv()
            ag(4, v, s, True).start()
            ag(5, v, s, True).start()

    def ag_a3(v):
        for s in range(2):
            for kind in (4, 5):
                ag(kind, v, s, False).wait_recv()
                ag(kind + 2, v, s, True).start()

    def ag_a4(v):
        for s in range(2):
            ag(6, v, s, False).wait_recv()
            ag(7, v, s, False).wait_recv()

    def rs(kind, j, s, o, sending):
        step = 1 if o == 0 else -1
        a, b = place[s]
        number = kind % 3
        direction = -step if number == 2 else step
        ssem, rsem = rs_s.at[kind, j, s, o], rs_r.at[kind, j, s, o]
        if kind < 3:
            two = pl.ds(2 * o, 2)
            src = sb.at[number, j, s, two]
            dst = ra.at[number, j, s, two]
            device = chip(axes[s][0], direction)
        else:
            eight = pl.ds(8 * o, 8)
            target = (at(b, 2), at(b, step), at(b, -step))[number]
            src = vf.at[j, s, target, eight]
            dst = rb.at[number, j, s, eight]
            device = chip(axes[s][1], direction)
        return remote(src, dst, ssem, rsem, device)

    def own_part(j, s, a, o):
        two = pl.ds(2 * o, 2)
        if s == 0:
            return part[j, a, two, :, cols[s]]
        return part[j, two, a, :, cols[s]]

    def rs_s0(j):
        for step in range(1, 8):
            og_copy(j, step, (col + 8 - step) % 8).wait_recv()
        lhs = og_all[j].reshape(16 * ROWS, D)

        @pl.loop(0, F // TILE, unroll=True)
        def _(n):
            at_n = pl.ds(pl.multiple_of(n * TILE, TILE), TILE)
            out = lax.dot_general(lhs, dw[at_n, :], NT, preferred_element_type=F32)
            part[j, :, :, :, at_n] = out.reshape(N, N, ROWS, TILE)

        for s in range(2):
            a = place[s][0]
            for o in range(2):
                step = 1 if o == 0 else -1
                two = pl.ds(2 * o, 2)
                sb[0, j, s, two] = own_part(j, s, at(a, 2), o).astype(BF16)
                rs(0, j, s, o, True).start()
        for s in range(2):
            a = place[s][0]
            for o in range(2):
                step = 1 if o == 0 else -1
                two = pl.ds(2 * o, 2)
                sb[2, j, s, two] = own_part(j, s, at(a, -step), o).astype(BF16)
                rs(2, j, s, o, True).start()

    def rs_s1(j):
        for s in range(2):
            a = place[s][0]
            for o in range(2):
                step = 1 if o == 0 else -1
                two = pl.ds(2 * o, 2)
                rs(0, j, s, o, False).wait_recv()
                total = own_part(j, s, at(a, step), o) + ra[0, j, s, two].astype(F32)
                sb[1, j, s, two] = total.astype(BF16)
                rs(1, j, s, o, True).start()

    def rs_s2(j):
        for s in range(2):
            a = place[s][0]
            for o in range(2):
                two = pl.ds(2 * o, 2)
                rs(2, j, s, o, False).wait_recv()
                rs(1, j, s, o, False).wait_recv()
                vf[j, s, two] = (
                    own_part(j, s, a, o)
                    + ra[1, j, s, two].astype(F32)
                    + ra[2, j, s, two].astype(F32)
                )
            for o in range(2):
                rs(3, j, s, o, True).start()
                rs(5, j, s, o, True).start()

    def rs_s3(j):
        for s in range(2):
            b = place[s][1]
            for o in range(2):
                step = 1 if o == 0 else -1
                eight = pl.ds(8 * o, 8)
                rs(3, j, s, o, False).wait_recv()
                vf[j, s, at(b, step), eight] = vf[j, s, at(b, step), eight] + rb[0, j, s, eight]
                rs(4, j, s, o, True).start()

    def pre(j, s):
        own = pl.ds(pl.multiple_of(j * ROWS, ROWS), ROWS)
        gate = gate_ref[own, cols[s]].astype(F32)
        up = up_ref[own, cols[s]].astype(F32)
        return gate, up, 1.0 / (1.0 + jnp.exp(-gate))

    def rs_s4(j):
        for s in range(2):
            b = place[s][1]
            for o in range(2):
                rs(5, j, s, o, False).wait_recv()
                rs(4, j, s, o, False).wait_recv()
            grad = vf[j, s, b] + rb[1, j, s] + rb[2, j, s]
            gate, up, sig = pre(j, s)
            first = slots(j)
            arr[first, y, x, :, cols[s]] = (grad * up * sig * (1.0 + gate * (1.0 - sig))).astype(BF16)
            arr[first + 1, y, x, :, cols[s]] = (grad * gate * sig).astype(BF16)
            ag(0, j, s, True).start()
            ag(1, j, s, True).start()

    def hidden(slot, j):
        for s in range(2):
            gate, up, sig = pre(j, s)
            arr[slot, y, x, :, cols[s]] = (gate * sig * up).astype(BF16)

    def ig_pair(j):
        return remote(ip.at[j, :, 1 - k], ri.at[j], ig_s.at[0, j], ig_r.at[0, j], (row, 2 * z + 1 - k))

    def ig_send(j, step):
        return remote(
            ip.at[j, at(z, step), k], rz.at[j, step - 1],
            ig_s.at[step, j], ig_r.at[step, j], (row, 2 * at(z, step) + k),
        )

    def ig_i0(j):
        first = slots(j)
        for n in range(D // TILE):
            at_n = pl.ds(n * TILE, TILE)
            out = lax.dot_general(
                arr[first].reshape(16 * ROWS, F), gw[at_n, :], NT, preferred_element_type=F32
            ) + lax.dot_general(
                arr[first + 1].reshape(16 * ROWS, F), uw[at_n, :], NT, preferred_element_type=F32
            )
            ip[j, :, :, :, :, at_n] = out.reshape(N, 2, 2, ROWS, TILE)
        ig_pair(j).start()

    def ig_i1(j):
        ig_pair(j).wait_recv()
        for step in (2, 1, 3, 0):
            t = at(z, step)
            ip[j, t, k] = ip[j, t, k] + ri[j, t]
            if step:
                ig_send(j, step).start()

    def ig_i2(j):
        for step in (1, 2, 3):
            ig_send(j, step).wait_recv()
        total = ip[j, z, k] + rz[j, 0] + rz[j, 1] + rz[j, 2]
        for half in range(2):
            own = pl.ds(pl.multiple_of(half * N * ROWS + j * ROWS, ROWS), ROWS)
            ig_ref[own, :] = total[half]

    def wg(j):
        first = slots(j)
        for ref, slot in ((gg_ref, first), (ug_ref, first + 1)):

            @pl.loop(0, F // TILE)
            def _(n):
                at_n = pl.ds(pl.multiple_of(n * TILE, TILE), TILE)
                rhs = arr[slot, :, :, :, at_n].reshape(16 * ROWS, TILE)
                out = jnp.dot(in_t[j], rhs, preferred_element_type=F32)

                ref[:, at_n] = jnp.where(j > 0, ref[:, at_n], 0.0) + out

    def turn(j):
        in_t[j] = in_all[j].reshape(16 * ROWS, D).T

    pl.semaphore_wait(barrier, 11)
    for j in range(N):
        for step in (4, 3, 5, 2, 6, 1, 7):
            og_copy(j, step, col).start()
    loads[2].wait()
    loads[3].wait()
    hidden(0, 0)
    hidden(1, 1)
    ag_a0(-6)
    for step in (4, 3, 5, 2, 6, 1, 7):
        in_copy(step, col).start()
    hidden(10, 2)
    hidden(11, 3)
    ag_a0(4)
    ag_a1(-6)
    loads[4].wait()

    def stage(t, number, count, call):
        j = t - number

        @pl.when((j >= 0) & (j < count))
        def _():
            call(j)

    def ag_stage(t, number, call):
        v = t - number

        @pl.when(((v >= 0) & (v < N)) | (v == N + 1))
        def _():
            call(v)

    def ag_sent(v):
        for s in range(2):
            for kind in range(8):
                ag(kind, v, s, True).wait_send()

    def sent(j):
        for s in range(2):
            for o in range(2):
                for kind in range(6):
                    rs(kind, j, s, o, True).wait_send()
        ag_sent(j)

    @pl.loop(0, 14)
    def _(t):
        stage(t, 4, N, rs_s4)
        stage(t, 3, N, rs_s3)
        stage(t, 2, N, rs_s2)
        stage(t, 1, N, rs_s1)
        stage(t, 0, N, rs_s0)

        @pl.when(t == 0)
        def _():
            ag_a2(-6)

        @pl.when(t == 1)
        def _():
            ag_a3(-6)

        @pl.when(t == 7)
        def _():
            loads[5].wait()
            loads[6].wait()

        ag_stage(t, 5, ag_a1)
        ag_stage(t, 6, ag_a2)
        ag_stage(t, 7, ag_a3)
        @pl.when(t == 7)
        def _():
            for step in range(1, 8):
                in_copy(step, (col + 8 - step) % 8).wait_recv()

        stage(t, 7, N, turn)

        stage(t, 9, N, ig_i1)
        @pl.when(t == 8)
        def _():
            ag_a4(-6)

        stage(t, 9, N, wg)

        @pl.when(t == 9)
        def _():
            for j in range(N):
                for step in range(1, 8):
                    og_copy(j, step, col).wait_send()
            for step in range(1, 8):
                in_copy(step, col).wait_send()
            ag_sent(-6)

        stage(t, 10, N, sent)
        stage(t, 8, N, ag_a4)
        stage(t, 8, N, ig_i0)
        stage(t, 10, N, ig_i2)

    ag_a4(4)
    for j in range(N):
        ig_pair(j).wait_send()
        for step in (1, 2, 3):
            ig_send(j, step).wait_send()
    ag_sent(4)


def exchange(out_grad, inputs, gate_pre, up_pre, gate_weight, up_weight, down_weight):
    vmem = pl.BlockSpec(memory_space=pltpu.VMEM)
    hbm = pl.BlockSpec(memory_space=pl.ANY)
    dma = pltpu.SemaphoreType.DMA
    return pl.pallas_call(
        _exchange,
        out_shape=(
            pltpu.VMEM((128, D), F32),
            pltpu.VMEM((D, F), F32),
            pltpu.VMEM((D, F), F32),
            pltpu.VMEM((12, N, N, ROWS, F), BF16),
            pltpu.VMEM((N, 16, ROWS, D), BF16),
        ),
        in_specs=[hbm] * 7,
        out_specs=(vmem,) * 5,
        scratch_shapes=[
            pltpu.VMEM((128, D), BF16),
            pltpu.VMEM((128, D), BF16),
            pltpu.VMEM((N * ROWS, F), BF16),
            pltpu.VMEM((N * ROWS, F), BF16),
            pltpu.VMEM((F, D), BF16),
            pltpu.VMEM((D, F), BF16),
            pltpu.VMEM((D, F), BF16),
            pltpu.VMEM((N, 16, ROWS, D), BF16),
            pltpu.VMEM((N, D, 16 * ROWS), BF16),
            pltpu.VMEM((N, N, N, ROWS, F), F32),
            pltpu.VMEM((3, N, 2, N, ROWS, HALF), BF16),
            pltpu.VMEM((3, N, 2, N, ROWS, HALF), BF16),
            pltpu.VMEM((N, 2, N, ROWS, HALF), F32),
            pltpu.VMEM((3, N, 2, ROWS, HALF), F32),
            pltpu.VMEM((N, N, 2, 2, ROWS, D), F32),
            pltpu.VMEM((N, N, 2, ROWS, D), F32),
            pltpu.VMEM((N, 3, 2, ROWS, D), F32),
            dma((7,)),
            dma((N, 7)),
            dma((N, 7)),
            dma((7,)),
            dma((7,)),
            dma((6, N, 2, 2)),
            dma((6, N, 2, 2)),
            dma((8, 6, 2)),
            dma((8, 6, 2)),
            dma((4, N)),
            dma((4, N)),
        ],
        compiler_params=pltpu.CompilerParams(
            collective_id=0, has_side_effects=True, vmem_limit_bytes=38 << 20
        ),
        cost_estimate=pl.CostEstimate(
            flops=6 * 1024 * D * F, bytes_accessed=20 << 20, transcendentals=64 * F
        ),
        name="exchange",
    )(out_grad, inputs, gate_pre, up_pre, gate_weight, up_weight, down_weight)


def _finish(ig, gg, ug, arr, og, ig_out, gg_out, ug_out, dg_out, total, sem, tile_sem):
    copies = [
        pltpu.make_async_copy(gg, gg_out, sem.at[0]),
        pltpu.make_async_copy(ug, ug_out, sem.at[1]),
        pltpu.make_async_copy(ig, ig_out, sem.at[2]),
    ]
    for copy in copies:
        copy.start()

    def tile_copy(n):
        at_n = pl.ds(pl.multiple_of(n * TILE, TILE), TILE)
        return pltpu.make_async_copy(total.at[at_n], dg_out.at[at_n], tile_sem.at[n])

    @pl.loop(0, F // TILE)
    def _(n):
        at_n = pl.ds(pl.multiple_of(n * TILE, TILE), TILE)
        out = None
        for slot, j in ((0, 0), (1, 1), (10, 2), (11, 3)):
            lhs = arr[slot, :, :, :, at_n].reshape(16 * ROWS, TILE)
            rhs = og[j].reshape(16 * ROWS, D)
            product = lax.dot_general(lhs, rhs, TN, preferred_element_type=F32)
            out = product if out is None else out + product
        total[at_n, :] = out
        tile_copy(n).start()

    @pl.loop(0, F // TILE)
    def _(n):
        tile_copy(n).wait()

    for copy in copies:
        copy.wait()


def finish(*values):
    values = [pltpu.with_memory_space_constraint(v, pltpu.VMEM) for v in values]
    return pl.pallas_call(
        _finish,
        out_shape=[pltpu.HBM(v.shape, v.dtype) for v in values[:3]] + [pltpu.HBM((F, D), F32)],
        in_specs=[pl.BlockSpec(memory_space=pltpu.VMEM)] * 5,
        out_specs=[pl.BlockSpec(memory_space=pl.ANY)] * 4,
        scratch_shapes=[
            pltpu.VMEM((F, D), F32),
            pltpu.SemaphoreType.DMA((3,)),
            pltpu.SemaphoreType.DMA((F // TILE,)),
        ],
        compiler_params=pltpu.CompilerParams(vmem_limit_bytes=12 << 20),
        name="finish",
    )(*values)


def body(inputs, out_grad, gate_pre, up_pre, gate_weight, up_weight, down_weight):
    values = exchange(out_grad, inputs, gate_pre, up_pre, gate_weight, up_weight, down_weight)
    return tuple(finish(*values))


def solution(mesh):
    in_specs = (
        P("col", "row"),
        P("col", "row"),
        P("row", "col"),
        P("row", "col"),
        P("row", "col"),
        P("row", "col"),
        P("col", "row"),
    )
    out_specs = (P("col", "row"), P("row", "col"), P("row", "col"), P("col", "row"))
    return jax.shard_map(body, mesh=mesh, in_specs=in_specs, out_specs=out_specs, check_vma=False)
```

```python
import jax
import jax.numpy as jnp
from jax import lax
from jax.experimental import pallas as pl
from jax.experimental.pallas import tpu as pltpu
from jax.sharding import PartitionSpec as P

MESH = pl.DeviceIdType.MESH
F32 = jnp.float32
BF16 = jnp.bfloat16
NT = (((1,), (1,)), ((), ()))
TN = (((0,), (0,)), ((), ()))
N = 4
ROWS = 16
D = 512
F = 1792
HALF = F // 2
TILE = 256


def _exchange(
    og_hbm, in_hbm, gate_hbm, up_hbm, gw_hbm, uw_hbm, dw_hbm,
    ig_ref, gg_ref, ug_ref, arr, og_all,
    og_ref, in_ref, gate_ref, up_ref, dw, gw, uw, in_all, in_t, part, sb, ra, vf, rb, ip, ri, rz,
    load_sem, og_s, og_r, in_s, in_r, rs_s, rs_r, ag_s, ag_r, ig_s, ig_r,
):
    row, col = lax.axis_index("row"), lax.axis_index("col")
    y, x = row // N, row % N
    z, k = col // 2, col % 2

    def at(base, step):
        return (base + (step + N)) % N

    def chip(axis, step):
        if axis == "y":
            return (at(y, step) * N + x, col)
        return (y * N + at(x, step), col)

    def column(step):
        return (row, (col + step) % 8)

    axes = (("y", "x"), ("x", "y"))
    place = ((y, x), (x, y))
    cols = (pl.ds(0, HALF), pl.ds(HALF, HALF))

    barrier = pltpu.get_barrier_semaphore()
    for axis in ("y", "x"):
        for step in (1, -1):
            pl.semaphore_signal(barrier, inc=1, device_id=chip(axis, step), device_id_type=MESH)
    for step in range(1, 8):
        pl.semaphore_signal(barrier, inc=1, device_id=column(step), device_id_type=MESH)

    loads = [
        pltpu.make_async_copy(og_hbm, og_ref, load_sem.at[3]),
        pltpu.make_async_copy(in_hbm, in_ref, load_sem.at[4]),
        pltpu.make_async_copy(gate_hbm, gate_ref, load_sem.at[5]),
        pltpu.make_async_copy(up_hbm, up_ref, load_sem.at[6]),
        pltpu.make_async_copy(dw_hbm, dw, load_sem.at[0]),
        pltpu.make_async_copy(gw_hbm, gw, load_sem.at[1]),
        pltpu.make_async_copy(uw_hbm, uw, load_sem.at[2]),
    ]
    for load in loads:
        load.start()

    loads[0].wait()
    loads[1].wait()
    for j in range(N):
        for half in range(2):
            own = pl.ds(half * N * ROWS + j * ROWS, ROWS)
            og_all[j, 2 * col + half] = og_ref[own, :]
            in_all[j, 2 * col + half] = in_ref[own, :]

    def remote(src, dst, ssem, rsem, device):
        return pltpu.make_async_remote_copy(
            src_ref=src, dst_ref=dst, send_sem=ssem, recv_sem=rsem,
            device_id=device, device_id_type=MESH,
        )

    def og_copy(j, step, origin):
        block = og_all.at[j, pl.ds(2 * origin, 2)]
        return remote(block, block, og_s.at[j, step - 1], og_r.at[j, step - 1], column(step))

    def in_copy(step, origin):
        block = in_all.at[:, pl.ds(2 * origin, 2)]
        return remote(block, block, in_s.at[step - 1], in_r.at[step - 1], column(step))

    def slots(v):
        return jnp.clip(2 + 2 * v, 0, 10)

    def item(v):
        return jnp.clip(1 + v, 0, 5)

    def block(s, first, count, b):
        a = place[s][0]
        if s == 0:
            return arr.at[pl.ds(first, count), a, b, :, cols[s]]
        return arr.at[pl.ds(first, count), b, a, :, cols[s]]

    def group(s, first, count, a):
        if s == 0:
            return arr.at[pl.ds(first, count), a, :, :, cols[s]]
        return arr.at[pl.ds(first, count), :, a, :, cols[s]]

    def ag(kind, v, s, sending):
        a, b = place[s]
        first = slots(v)
        step = 1 if kind % 2 == 0 else -1
        axis = axes[s][1] if kind < 4 else axes[s][0]
        here = b if kind < 4 else a
        if kind in (0, 1, 4, 5):
            lead, count = first, 2
            origin = here if sending else at(here, -step)
        else:
            lead, count = first + (0 if step == 1 else 1), 1
            origin = at(here, -step) if sending else at(here, 2)
        view = block(s, lead, count, origin) if kind < 4 else group(s, lead, count, origin)
        return remote(
            view, view, ag_s.at[kind, item(v), s], ag_r.at[kind, item(v), s], chip(axis, step)
        )

    def ag_a0(v):
        for s in range(2):
            ag(0, v, s, True).start()
            ag(1, v, s, True).start()

    def ag_a1(v):
        for s in range(2):
            for kind in (0, 1):
                ag(kind, v, s, False).wait_recv()
                ag(kind + 2, v, s, True).start()

    def ag_a2(v):
        for s in range(2):
            ag(2, v, s, False).wait_recv()
            ag(3, v, s, False).wait_recv()
            ag(4, v, s, True).start()
            ag(5, v, s, True).start()

    def ag_a3(v):
        for s in range(2):
            for kind in (4, 5):
                ag(kind, v, s, False).wait_recv()
                ag(kind + 2, v, s, True).start()

    def ag_a4(v):
        for s in range(2):
            ag(6, v, s, False).wait_recv()
            ag(7, v, s, False).wait_recv()

    def rs(kind, j, s, o, sending):
        step = 1 if o == 0 else -1
        a, b = place[s]
        number = kind % 3
        direction = -step if number == 2 else step
        ssem, rsem = rs_s.at[kind, j, s, o], rs_r.at[kind, j, s, o]
        if kind < 3:
            two = pl.ds(2 * o, 2)
            src = sb.at[number, j, s, two]
            dst = ra.at[number, j, s, two]
            device = chip(axes[s][0], direction)
        else:
            eight = pl.ds(8 * o, 8)
            target = (at(b, 2), at(b, step), at(b, -step))[number]
            src = vf.at[j, s, target, eight]
            dst = rb.at[number, j, s, eight]
            device = chip(axes[s][1], direction)
        return remote(src, dst, ssem, rsem, device)

    def own_part(j, s, a, o):
        two = pl.ds(2 * o, 2)
        if s == 0:
            return part[j, a, two, :, cols[s]]
        return part[j, two, a, :, cols[s]]

    def rs_s0(j):
        for step in range(1, 8):
            og_copy(j, step, (col + 8 - step) % 8).wait_recv()
        lhs = og_all[j].reshape(16 * ROWS, D)

        @pl.loop(0, F // TILE, unroll=True)
        def _(n):
            at_n = pl.ds(pl.multiple_of(n * TILE, TILE), TILE)
            out = lax.dot_general(lhs, dw[at_n, :], NT, preferred_element_type=F32)
            part[j, :, :, :, at_n] = out.reshape(N, N, ROWS, TILE)

        for s in range(2):
            a = place[s][0]
            for o in range(2):
                step = 1 if o == 0 else -1
                two = pl.ds(2 * o, 2)
                sb[0, j, s, two] = own_part(j, s, at(a, 2), o).astype(BF16)
                rs(0, j, s, o, True).start()
        for s in range(2):
            a = place[s][0]
            for o in range(2):
                step = 1 if o == 0 else -1
                two = pl.ds(2 * o, 2)
                sb[2, j, s, two] = own_part(j, s, at(a, -step), o).astype(BF16)
                rs(2, j, s, o, True).start()

    def rs_s1(j):
        for s in range(2):
            a = place[s][0]
            for o in range(2):
                step = 1 if o == 0 else -1
                two = pl.ds(2 * o, 2)
                rs(0, j, s, o, False).wait_recv()
                total = own_part(j, s, at(a, step), o) + ra[0, j, s, two].astype(F32)
                sb[1, j, s, two] = total.astype(BF16)
                rs(1, j, s, o, True).start()

    def rs_s2(j):
        for s in range(2):
            a = place[s][0]
            for o in range(2):
                two = pl.ds(2 * o, 2)
                rs(2, j, s, o, False).wait_recv()
                rs(1, j, s, o, False).wait_recv()
                vf[j, s, two] = (
                    own_part(j, s, a, o)
                    + ra[1, j, s, two].astype(F32)
                    + ra[2, j, s, two].astype(F32)
                )
            for o in range(2):
                rs(3, j, s, o, True).start()
                rs(5, j, s, o, True).start()

    def rs_s3(j):
        for s in range(2):
            b = place[s][1]
            for o in range(2):
                step = 1 if o == 0 else -1
                eight = pl.ds(8 * o, 8)
                rs(3, j, s, o, False).wait_recv()
                vf[j, s, at(b, step), eight] = vf[j, s, at(b, step), eight] + rb[0, j, s, eight]
                rs(4, j, s, o, True).start()

    def pre(j, s):
        own = pl.ds(pl.multiple_of(j * ROWS, ROWS), ROWS)
        gate = gate_ref[own, cols[s]].astype(F32)
        up = up_ref[own, cols[s]].astype(F32)
        return gate, up, 1.0 / (1.0 + jnp.exp(-gate))

    def rs_s4(j):
        for s in range(2):
            b = place[s][1]
            for o in range(2):
                rs(5, j, s, o, False).wait_recv()
                rs(4, j, s, o, False).wait_recv()
            grad = vf[j, s, b] + rb[1, j, s] + rb[2, j, s]
            gate, up, sig = pre(j, s)
            first = slots(j)
            arr[first, y, x, :, cols[s]] = (grad * up * sig * (1.0 + gate * (1.0 - sig))).astype(BF16)
            arr[first + 1, y, x, :, cols[s]] = (grad * gate * sig).astype(BF16)
            ag(0, j, s, True).start()
            ag(1, j, s, True).start()

    def hidden(slot, j):
        for s in range(2):
            gate, up, sig = pre(j, s)
            arr[slot, y, x, :, cols[s]] = (gate * sig * up).astype(BF16)

    def ig_pair(j):
        return remote(ip.at[j, :, 1 - k], ri.at[j], ig_s.at[0, j], ig_r.at[0, j], (row, 2 * z + 1 - k))

    def ig_send(j, step):
        return remote(
            ip.at[j, at(z, step), k], rz.at[j, step - 1],
            ig_s.at[step, j], ig_r.at[step, j], (row, 2 * at(z, step) + k),
        )

    def ig_i0(j):
        first = slots(j)
        for n in range(D // TILE):
            at_n = pl.ds(n * TILE, TILE)
            out = lax.dot_general(
                arr[first].reshape(16 * ROWS, F), gw[at_n, :], NT, preferred_element_type=F32
            ) + lax.dot_general(
                arr[first + 1].reshape(16 * ROWS, F), uw[at_n, :], NT, preferred_element_type=F32
            )
            ip[j, :, :, :, :, at_n] = out.reshape(N, 2, 2, ROWS, TILE)
        ig_pair(j).start()

    def ig_i1(j):
        ig_pair(j).wait_recv()
        for step in (2, 1, 3, 0):
            t = at(z, step)
            ip[j, t, k] = ip[j, t, k] + ri[j, t]
            if step:
                ig_send(j, step).start()

    def ig_i2(j):
        for step in (1, 2, 3):
            ig_send(j, step).wait_recv()
        total = ip[j, z, k] + rz[j, 0] + rz[j, 1] + rz[j, 2]
        for half in range(2):
            own = pl.ds(pl.multiple_of(half * N * ROWS + j * ROWS, ROWS), ROWS)
            ig_ref[own, :] = total[half]

    def wg(j):
        first = slots(j)
        @pl.loop(0, F // TILE)
        def _(n):
            at_n = pl.ds(pl.multiple_of(n * TILE, TILE), TILE)
            for ref, slot in ((gg_ref, first), (ug_ref, first + 1)):
                rhs = arr[slot, :, :, :, at_n].reshape(16 * ROWS, TILE)
                out = jnp.dot(in_t[j], rhs, preferred_element_type=F32)
                ref[:, at_n] = jnp.where(j > 0, ref[:, at_n], 0.0) + out

    def turn(j):
        in_t[j] = in_all[j].reshape(16 * ROWS, D).T

    pl.semaphore_wait(barrier, 11)
    for j in range(N):
        for step in (4, 3, 5, 2, 6, 1, 7):
            og_copy(j, step, col).start()
    loads[2].wait()
    loads[3].wait()
    hidden(0, 0)
    hidden(1, 1)
    ag_a0(-6)
    for step in (4, 3, 5, 2, 6, 1, 7):
        in_copy(step, col).start()
    hidden(10, 2)
    hidden(11, 3)
    ag_a0(4)
    ag_a1(-6)
    loads[4].wait()

    def stage(t, number, count, call):
        j = t - number

        @pl.when((j >= 0) & (j < count))
        def _():
            call(j)

    def ag_sent(v):
        for s in range(2):
            for kind in range(8):
                ag(kind, v, s, True).wait_send()

    def sent(j):
        for s in range(2):
            for o in range(2):
                for kind in range(6):
                    rs(kind, j, s, o, True).wait_send()
        ag_sent(j)

    def once(t, number, *calls):
        @pl.when(t == number)
        def _():
            for call, v in calls:
                call(v)

    def weights_here(_):
        loads[5].wait()
        loads[6].wait()

    def inputs_here(_):
        for step in range(1, 8):
            in_copy(step, (col + 8 - step) % 8).wait_recv()

    def gathered_sent(_):
        for j in range(N):
            for step in range(1, 8):
                og_copy(j, step, col).wait_send()
        for step in range(1, 8):
            in_copy(step, col).wait_send()
        ag_sent(-6)

    @pl.loop(0, 14)
    def _(t):
        once(t, 9, (weights_here, 0))
        stage(t, 9, N, ig_i0)
        stage(t, 6, N, ag_a2)
        once(t, 6, (inputs_here, 0))
        stage(t, 6, N, turn)
        once(t, 7, (ag_a4, -6))

        @pl.when((t == 10) | (t == 13))
        def _():
            wg((t - 10) // 3)

        stage(t, 5, N, ag_a1)
        stage(t, 0, N, rs_s0)
        once(t, 0, (ag_a1, 4))
        stage(t, 1, N, rs_s1)
        stage(t, 10, N, ig_i1)
        stage(t, 2, N, rs_s2)
        stage(t, 3, N, rs_s3)
        once(t, 6, (ag_a3, -6))
        stage(t, 7, N, ag_a3)
        stage(t, 4, N, rs_s4)
        once(t, 10, (ag_a2, 4))
        once(t, 4, (ag_a2, -6))
        stage(t, 8, N, ag_a4)
        once(t, 9, (gathered_sent, 0))
        stage(t, 10, N - 1, sent)

    ag_a3(4)

    @pl.loop(2, N)
    def _(j):
        wg(j)

    sent(3)

    @pl.loop(0, N)
    def _(j):
        ig_i2(j)

    ag_a4(4)
    for j in range(N):
        ig_pair(j).wait_send()
        for step in (1, 2, 3):
            ig_send(j, step).wait_send()
    ag_sent(4)


def exchange(out_grad, inputs, gate_pre, up_pre, gate_weight, up_weight, down_weight):
    vmem = pl.BlockSpec(memory_space=pltpu.VMEM)
    hbm = pl.BlockSpec(memory_space=pl.ANY)
    dma = pltpu.SemaphoreType.DMA
    return pl.pallas_call(
        _exchange,
        out_shape=(
            pltpu.VMEM((128, D), F32),
            pltpu.VMEM((D, F), F32),
            pltpu.VMEM((D, F), F32),
            pltpu.VMEM((12, N, N, ROWS, F), BF16),
            pltpu.VMEM((N, 16, ROWS, D), BF16),
        ),
        in_specs=[hbm] * 7,
        out_specs=(vmem,) * 5,
        scratch_shapes=[
            pltpu.VMEM((128, D), BF16),
            pltpu.VMEM((128, D), BF16),
            pltpu.VMEM((N * ROWS, F), BF16),
            pltpu.VMEM((N * ROWS, F), BF16),
            pltpu.VMEM((F, D), BF16),
            pltpu.VMEM((D, F), BF16),
            pltpu.VMEM((D, F), BF16),
            pltpu.VMEM((N, 16, ROWS, D), BF16),
            pltpu.VMEM((N, D, 16 * ROWS), BF16),
            pltpu.VMEM((N, N, N, ROWS, F), F32),
            pltpu.VMEM((3, N, 2, N, ROWS, HALF), BF16),
            pltpu.VMEM((3, N, 2, N, ROWS, HALF), BF16),
            pltpu.VMEM((N, 2, N, ROWS, HALF), F32),
            pltpu.VMEM((3, N, 2, ROWS, HALF), F32),
            pltpu.VMEM((N, N, 2, 2, ROWS, D), F32),
            pltpu.VMEM((N, N, 2, ROWS, D), F32),
            pltpu.VMEM((N, 3, 2, ROWS, D), F32),
            dma((7,)),
            dma((N, 7)),
            dma((N, 7)),
            dma((7,)),
            dma((7,)),
            dma((6, N, 2, 2)),
            dma((6, N, 2, 2)),
            dma((8, 6, 2)),
            dma((8, 6, 2)),
            dma((4, N)),
            dma((4, N)),
        ],
        compiler_params=pltpu.CompilerParams(
            collective_id=0, has_side_effects=True, vmem_limit_bytes=38 << 20
        ),
        cost_estimate=pl.CostEstimate(
            flops=6 * 1024 * D * F, bytes_accessed=20 << 20, transcendentals=64 * F
        ),
        name="exchange",
    )(out_grad, inputs, gate_pre, up_pre, gate_weight, up_weight, down_weight)


def _finish(ig, gg, ug, arr, og, ig_out, gg_out, ug_out, dg_out, total, sem, tile_sem):
    copies = [
        pltpu.make_async_copy(gg, gg_out, sem.at[0]),
        pltpu.make_async_copy(ug, ug_out, sem.at[1]),
        pltpu.make_async_copy(ig, ig_out, sem.at[2]),
    ]
    for copy in copies:
        copy.start()

    def tile_copy(n):
        at_n = pl.ds(pl.multiple_of(n * TILE, TILE), TILE)
        return pltpu.make_async_copy(total.at[at_n], dg_out.at[at_n], tile_sem.at[n])

    @pl.loop(0, F // TILE)
    def _(n):
        at_n = pl.ds(pl.multiple_of(n * TILE, TILE), TILE)
        out = None
        for slot, j in ((0, 0), (1, 1), (10, 2), (11, 3)):
            lhs = arr[slot, :, :, :, at_n].reshape(16 * ROWS, TILE)
            rhs = og[j].reshape(16 * ROWS, D)
            product = lax.dot_general(lhs, rhs, TN, preferred_element_type=F32)
            out = product if out is None else out + product
        total[at_n, :] = out
        tile_copy(n).start()

    @pl.loop(0, F // TILE)
    def _(n):
        tile_copy(n).wait()

    for copy in copies:
        copy.wait()


def finish(*values):
    values = [pltpu.with_memory_space_constraint(v, pltpu.VMEM) for v in values]
    return pl.pallas_call(
        _finish,
        out_shape=[pltpu.HBM(v.shape, v.dtype) for v in values[:3]] + [pltpu.HBM((F, D), F32)],
        in_specs=[pl.BlockSpec(memory_space=pltpu.VMEM)] * 5,
        out_specs=[pl.BlockSpec(memory_space=pl.ANY)] * 4,
        scratch_shapes=[
            pltpu.VMEM((F, D), F32),
            pltpu.SemaphoreType.DMA((3,)),
            pltpu.SemaphoreType.DMA((F // TILE,)),
        ],
        compiler_params=pltpu.CompilerParams(vmem_limit_bytes=12 << 20),
        name="finish",
    )(*values)


def body(inputs, out_grad, gate_pre, up_pre, gate_weight, up_weight, down_weight):
    values = exchange(out_grad, inputs, gate_pre, up_pre, gate_weight, up_weight, down_weight)
    return tuple(finish(*values))


def solution(mesh):
    in_specs = (
        P("col", "row"),
        P("col", "row"),
        P("row", "col"),
        P("row", "col"),
        P("row", "col"),
        P("row", "col"),
        P("col", "row"),
    )
    out_specs = (P("col", "row"), P("row", "col"), P("row", "col"), P("col", "row"))
    return jax.shard_map(body, mesh=mesh, in_specs=in_specs, out_specs=out_specs, check_vma=False)
```

```python
import jax
import jax.numpy as jnp
from jax import lax
from jax.experimental import pallas as pl
from jax.experimental.pallas import tpu as pltpu
from jax.sharding import PartitionSpec as P

MESH = pl.DeviceIdType.MESH
F32 = jnp.float32
BF16 = jnp.bfloat16
NT = (((1,), (1,)), ((), ()))
TN = (((0,), (0,)), ((), ()))
N = 4
ROWS = 16
D = 512
F = 1792
HALF = F // 2
TILE = 256


def _exchange(
    og_hbm, in_hbm, gate_hbm, up_hbm, gw_hbm, uw_hbm, dw_hbm,
    ig_ref, gg_ref, ug_ref, arr, og_all,
    og_ref, in_ref, gate_ref, up_ref, dw, gw, uw, in_all, in_t, part, sb, ra, vf, rb, ip, ri, rz,
    load_sem, og_s, og_r, in_s, in_r, rs_s, rs_r, ag_s, ag_r, ig_s, ig_r,
):
    row, col = lax.axis_index("row"), lax.axis_index("col")
    y, x = row // N, row % N
    z, k = col // 2, col % 2

    def at(base, step):
        return (base + (step + N)) % N

    def chip(axis, step):
        if axis == "y":
            return (at(y, step) * N + x, col)
        return (y * N + at(x, step), col)

    def column(step):
        return (row, (col + step) % 8)

    axes = (("y", "x"), ("x", "y"))
    place = ((y, x), (x, y))
    cols = (pl.ds(0, HALF), pl.ds(HALF, HALF))

    barrier = pltpu.get_barrier_semaphore()
    for axis in ("y", "x"):
        for step in (1, -1):
            pl.semaphore_signal(barrier, inc=1, device_id=chip(axis, step), device_id_type=MESH)
    for step in range(1, 8):
        pl.semaphore_signal(barrier, inc=1, device_id=column(step), device_id_type=MESH)

    loads = [
        pltpu.make_async_copy(og_hbm, og_ref, load_sem.at[3]),
        pltpu.make_async_copy(in_hbm, in_ref, load_sem.at[4]),
        pltpu.make_async_copy(gate_hbm, gate_ref, load_sem.at[5]),
        pltpu.make_async_copy(up_hbm, up_ref, load_sem.at[6]),
        pltpu.make_async_copy(dw_hbm, dw, load_sem.at[0]),
        pltpu.make_async_copy(gw_hbm, gw, load_sem.at[1]),
        pltpu.make_async_copy(uw_hbm, uw, load_sem.at[2]),
    ]
    for load in loads:
        load.start()

    loads[0].wait()
    loads[1].wait()
    for j in range(N):
        for half in range(2):
            own = pl.ds(half * N * ROWS + j * ROWS, ROWS)
            og_all[j, 2 * col + half] = og_ref[own, :]
            in_all[j, 2 * col + half] = in_ref[own, :]

    def remote(src, dst, ssem, rsem, device):
        return pltpu.make_async_remote_copy(
            src_ref=src, dst_ref=dst, send_sem=ssem, recv_sem=rsem,
            device_id=device, device_id_type=MESH,
        )

    def og_copy(j, step, origin):
        block = og_all.at[j, pl.ds(2 * origin, 2)]
        return remote(block, block, og_s.at[j, step - 1], og_r.at[j, step - 1], column(step))

    def in_copy(step, origin):
        block = in_all.at[:, pl.ds(2 * origin, 2)]
        return remote(block, block, in_s.at[step - 1], in_r.at[step - 1], column(step))

    def slots(v):
        return jnp.clip(2 + 2 * v, 0, 10)

    def item(v):
        return jnp.clip(1 + v, 0, 5)

    def block(s, first, count, b):
        a = place[s][0]
        if s == 0:
            return arr.at[pl.ds(first, count), a, b, :, cols[s]]
        return arr.at[pl.ds(first, count), b, a, :, cols[s]]

    def group(s, first, count, a):
        if s == 0:
            return arr.at[pl.ds(first, count), a, :, :, cols[s]]
        return arr.at[pl.ds(first, count), :, a, :, cols[s]]

    def ag(kind, v, s, sending):
        a, b = place[s]
        first = slots(v)
        step = 1 if kind % 2 == 0 else -1
        axis = axes[s][1] if kind < 4 else axes[s][0]
        here = b if kind < 4 else a
        if kind in (0, 1, 4, 5):
            lead, count = first, 2
            origin = here if sending else at(here, -step)
        else:
            lead, count = first + (0 if step == 1 else 1), 1
            origin = at(here, -step) if sending else at(here, 2)
        view = block(s, lead, count, origin) if kind < 4 else group(s, lead, count, origin)
        return remote(
            view, view, ag_s.at[kind, item(v), s], ag_r.at[kind, item(v), s], chip(axis, step)
        )

    def ag_a0(v):
        for s in range(2):
            ag(0, v, s, True).start()
            ag(1, v, s, True).start()

    def ag_a1(v):
        for s in range(2):
            for kind in (0, 1):
                ag(kind, v, s, False).wait_recv()
                ag(kind + 2, v, s, True).start()

    def ag_a2(v):
        for s in range(2):
            ag(2, v, s, False).wait_recv()
            ag(3, v, s, False).wait_recv()
            ag(4, v, s, True).start()
            ag(5, v, s, True).start()

    def ag_a3(v):
        for s in range(2):
            for kind in (4, 5):
                ag(kind, v, s, False).wait_recv()
                ag(kind + 2, v, s, True).start()

    def ag_a4(v):
        for s in range(2):
            ag(6, v, s, False).wait_recv()
            ag(7, v, s, False).wait_recv()

    def rs(kind, j, s, o, sending):
        step = 1 if o == 0 else -1
        a, b = place[s]
        number = kind % 3
        direction = -step if number == 2 else step
        ssem, rsem = rs_s.at[kind, j, s, o], rs_r.at[kind, j, s, o]
        if kind < 3:
            two = pl.ds(2 * o, 2)
            src = sb.at[number, j, s, two]
            dst = ra.at[number, j, s, two]
            device = chip(axes[s][0], direction)
        else:
            eight = pl.ds(8 * o, 8)
            target = (at(b, 2), at(b, step), at(b, -step))[number]
            src = vf.at[j, s, target, eight]
            dst = rb.at[number, j, s, eight]
            device = chip(axes[s][1], direction)
        return remote(src, dst, ssem, rsem, device)

    def own_part(j, s, a, o):
        two = pl.ds(2 * o, 2)
        if s == 0:
            return part[j, a, two, :, cols[s]]
        return part[j, two, a, :, cols[s]]

    def rs_s0(j):
        for step in range(1, 8):
            og_copy(j, step, (col + 8 - step) % 8).wait_recv()
        lhs = og_all[j].reshape(16 * ROWS, D)

        @pl.loop(0, F // TILE, unroll=True)
        def _(n):
            at_n = pl.ds(pl.multiple_of(n * TILE, TILE), TILE)
            out = lax.dot_general(lhs, dw[at_n, :], NT, preferred_element_type=F32)
            part[j, :, :, :, at_n] = out.reshape(N, N, ROWS, TILE)

        for s in range(2):
            a = place[s][0]
            for o in range(2):
                step = 1 if o == 0 else -1
                two = pl.ds(2 * o, 2)
                sb[0, j, s, two] = own_part(j, s, at(a, 2), o).astype(BF16)
                rs(0, j, s, o, True).start()
        for s in range(2):
            a = place[s][0]
            for o in range(2):
                step = 1 if o == 0 else -1
                two = pl.ds(2 * o, 2)
                sb[2, j, s, two] = own_part(j, s, at(a, -step), o).astype(BF16)
                rs(2, j, s, o, True).start()

    def rs_s1(j):
        for s in range(2):
            a = place[s][0]
            for o in range(2):
                step = 1 if o == 0 else -1
                two = pl.ds(2 * o, 2)
                rs(0, j, s, o, False).wait_recv()
                total = own_part(j, s, at(a, step), o) + ra[0, j, s, two].astype(F32)
                sb[1, j, s, two] = total.astype(BF16)
                rs(1, j, s, o, True).start()

    def rs_s2(j):
        for s in range(2):
            a = place[s][0]
            for o in range(2):
                two = pl.ds(2 * o, 2)
                rs(2, j, s, o, False).wait_recv()
                rs(1, j, s, o, False).wait_recv()
                vf[j, s, two] = (
                    own_part(j, s, a, o)
                    + ra[1, j, s, two].astype(F32)
                    + ra[2, j, s, two].astype(F32)
                )
            for o in range(2):
                rs(3, j, s, o, True).start()
                rs(5, j, s, o, True).start()

    def rs_s3(j):
        for s in range(2):
            b = place[s][1]
            for o in range(2):
                step = 1 if o == 0 else -1
                eight = pl.ds(8 * o, 8)
                rs(3, j, s, o, False).wait_recv()
                vf[j, s, at(b, step), eight] = vf[j, s, at(b, step), eight] + rb[0, j, s, eight]
                rs(4, j, s, o, True).start()

    def pre(j, s):
        own = pl.ds(pl.multiple_of(j * ROWS, ROWS), ROWS)
        gate = gate_ref[own, cols[s]].astype(F32)
        up = up_ref[own, cols[s]].astype(F32)
        return gate, up, 1.0 / (1.0 + jnp.exp(-gate))

    def rs_s4(j):
        for s in range(2):
            b = place[s][1]
            for o in range(2):
                rs(5, j, s, o, False).wait_recv()
                rs(4, j, s, o, False).wait_recv()
            grad = vf[j, s, b] + rb[1, j, s] + rb[2, j, s]
            gate, up, sig = pre(j, s)
            first = slots(j)
            arr[first, y, x, :, cols[s]] = (grad * up * sig * (1.0 + gate * (1.0 - sig))).astype(BF16)
            arr[first + 1, y, x, :, cols[s]] = (grad * gate * sig).astype(BF16)
            ag(0, j, s, True).start()
            ag(1, j, s, True).start()

    def hidden(slot, j):
        for s in range(2):
            gate, up, sig = pre(j, s)
            arr[slot, y, x, :, cols[s]] = (gate * sig * up).astype(BF16)

    def ig_pair(j):
        return remote(ip.at[j, :, 1 - k], ri.at[j], ig_s.at[0, j], ig_r.at[0, j], (row, 2 * z + 1 - k))

    def ig_send(j, step):
        return remote(
            ip.at[j, at(z, step), k], rz.at[j, step - 1],
            ig_s.at[step, j], ig_r.at[step, j], (row, 2 * at(z, step) + k),
        )

    def ig_i0(j):
        first = slots(j)
        for n in range(D // TILE):
            at_n = pl.ds(n * TILE, TILE)
            out = lax.dot_general(
                arr[first].reshape(16 * ROWS, F), gw[at_n, :], NT, preferred_element_type=F32
            ) + lax.dot_general(
                arr[first + 1].reshape(16 * ROWS, F), uw[at_n, :], NT, preferred_element_type=F32
            )
            ip[j, :, :, :, :, at_n] = out.reshape(N, 2, 2, ROWS, TILE)
        ig_pair(j).start()

    def ig_i1(j):
        ig_pair(j).wait_recv()
        for step in (2, 1, 3, 0):
            t = at(z, step)
            ip[j, t, k] = ip[j, t, k] + ri[j, t]
            if step:
                ig_send(j, step).start()

    def ig_i2(j):
        for step in (1, 2, 3):
            ig_send(j, step).wait_recv()
        total = ip[j, z, k] + rz[j, 0] + rz[j, 1] + rz[j, 2]
        for half in range(2):
            own = pl.ds(pl.multiple_of(half * N * ROWS + j * ROWS, ROWS), ROWS)
            ig_ref[own, :] = total[half]

    def wg(j):
        first = slots(j)
        @pl.loop(0, F // TILE)
        def _(n):
            at_n = pl.ds(pl.multiple_of(n * TILE, TILE), TILE)
            for ref, slot in ((gg_ref, first), (ug_ref, first + 1)):
                rhs = arr[slot, :, :, :, at_n].reshape(16 * ROWS, TILE)
                out = jnp.dot(in_t[j], rhs, preferred_element_type=F32)
                ref[:, at_n] = jnp.where(j > 0, ref[:, at_n], 0.0) + out

    def turn(j):
        in_t[j] = in_all[j].reshape(16 * ROWS, D).T

    pl.semaphore_wait(barrier, 11)
    for j in range(N):
        for step in (4, 3, 5, 2, 6, 1, 7):
            og_copy(j, step, col).start()
    loads[2].wait()
    loads[3].wait()
    hidden(0, 0)
    hidden(1, 1)
    ag_a0(-6)
    for step in (4, 3, 5, 2, 6, 1, 7):
        in_copy(step, col).start()
    hidden(10, 2)
    hidden(11, 3)
    ag_a0(4)
    ag_a1(-6)
    loads[4].wait()

    def stage(t, number, count, call):
        j = t - number

        @pl.when((j >= 0) & (j < count))
        def _():
            call(j)

    def ag_sent(v):
        for s in range(2):
            for kind in range(8):
                ag(kind, v, s, True).wait_send()

    def sent(j):
        for s in range(2):
            for o in range(2):
                for kind in range(6):
                    rs(kind, j, s, o, True).wait_send()
        ag_sent(j)

    def once(t, number, *calls):
        @pl.when(t == number)
        def _():
            for call, v in calls:
                call(v)

    def weights_here(_):
        loads[5].wait()
        loads[6].wait()

    def inputs_here(_):
        for step in range(1, 8):
            in_copy(step, (col + 8 - step) % 8).wait_recv()

    def gathered_sent(_):
        for j in range(N):
            for step in range(1, 8):
                og_copy(j, step, col).wait_send()
        for step in range(1, 8):
            in_copy(step, col).wait_send()
        ag_sent(-6)

    @pl.loop(0, 14)
    def _(t):
        once(t, 9, (weights_here, 0))
        stage(t, 9, N, ig_i0)
        stage(t, 6, N, ag_a2)
        once(t, 6, (inputs_here, 0))
        stage(t, 6, N, turn)
        once(t, 7, (ag_a4, -6))

        @pl.when((t == 10) | (t == 13))
        def _():
            wg((t - 10) // 3)

        stage(t, 5, N, ag_a1)
        stage(t, 0, N, rs_s0)
        once(t, 0, (ag_a1, 4))
        stage(t, 1, N, rs_s1)
        stage(t, 10, N, ig_i1)
        stage(t, 2, N, rs_s2)
        stage(t, 3, N, rs_s3)
        once(t, 6, (ag_a3, -6))
        stage(t, 7, N, ag_a3)
        stage(t, 4, N, rs_s4)
        once(t, 10, (ag_a2, 4))
        once(t, 4, (ag_a2, -6))
        stage(t, 8, N, ag_a4)
        once(t, 9, (gathered_sent, 0))
        stage(t, 10, N - 1, sent)

    ag_a3(4)

    @pl.loop(2, N)
    def _(j):
        wg(j)

    sent(3)

    @pl.loop(0, N)
    def _(j):
        ig_i2(j)

    ag_a4(4)
    for j in range(N):
        ig_pair(j).wait_send()
        for step in (1, 2, 3):
            ig_send(j, step).wait_send()
    ag_sent(4)


def exchange(out_grad, inputs, gate_pre, up_pre, gate_weight, up_weight, down_weight):
    vmem = pl.BlockSpec(memory_space=pltpu.VMEM)
    hbm = pl.BlockSpec(memory_space=pl.ANY)
    dma = pltpu.SemaphoreType.DMA
    return pl.pallas_call(
        _exchange,
        out_shape=(
            pltpu.VMEM((128, D), F32),
            pltpu.VMEM((D, F), F32),
            pltpu.VMEM((D, F), F32),
            pltpu.VMEM((12, N, N, ROWS, F), BF16),
            pltpu.VMEM((N, 16, ROWS, D), BF16),
        ),
        in_specs=[hbm] * 7,
        out_specs=(vmem,) * 5,
        scratch_shapes=[
            pltpu.VMEM((128, D), BF16),
            pltpu.VMEM((128, D), BF16),
            pltpu.VMEM((N * ROWS, F), BF16),
            pltpu.VMEM((N * ROWS, F), BF16),
            pltpu.VMEM((F, D), BF16),
            pltpu.VMEM((D, F), BF16),
            pltpu.VMEM((D, F), BF16),
            pltpu.VMEM((N, 16, ROWS, D), BF16),
            pltpu.VMEM((N, D, 16 * ROWS), BF16),
            pltpu.VMEM((N, N, N, ROWS, F), F32),
            pltpu.VMEM((3, N, 2, N, ROWS, HALF), BF16),
            pltpu.VMEM((3, N, 2, N, ROWS, HALF), BF16),
            pltpu.VMEM((N, 2, N, ROWS, HALF), F32),
            pltpu.VMEM((3, N, 2, ROWS, HALF), F32),
            pltpu.VMEM((N, N, 2, 2, ROWS, D), F32),
            pltpu.VMEM((N, N, 2, ROWS, D), F32),
            pltpu.VMEM((N, 3, 2, ROWS, D), F32),
            dma((7,)),
            dma((N, 7)),
            dma((N, 7)),
            dma((7,)),
            dma((7,)),
            dma((6, N, 2, 2)),
            dma((6, N, 2, 2)),
            dma((8, 6, 2)),
            dma((8, 6, 2)),
            dma((4, N)),
            dma((4, N)),
        ],
        compiler_params=pltpu.CompilerParams(
            collective_id=0, has_side_effects=True, vmem_limit_bytes=38 << 20
        ),
        cost_estimate=pl.CostEstimate(
            flops=6 * 1024 * D * F, bytes_accessed=20 << 20, transcendentals=64 * F
        ),
        name="exchange",
    )(out_grad, inputs, gate_pre, up_pre, gate_weight, up_weight, down_weight)


def _finish(ig, gg, ug, arr, og, ig_out, gg_out, ug_out, dg_out, total, sem, tile_sem):
    copies = [
        pltpu.make_async_copy(src.at[part], dst.at[part], sem.at[i, p])
        for p, part in enumerate(pl.ds(128 * p, 128) for p in range(N))
        for i, (src, dst) in enumerate(((gg, gg_out), (ug, ug_out)))
    ]
    copies.append(pltpu.make_async_copy(ig, ig_out, sem.at[2, 0]))
    for copy in copies:
        copy.start()

    def tile_copy(n):
        at_n = pl.ds(pl.multiple_of(n * TILE, TILE), TILE)
        return pltpu.make_async_copy(total.at[at_n], dg_out.at[at_n], tile_sem.at[n])

    @pl.loop(0, F // TILE)
    def _(n):
        at_n = pl.ds(pl.multiple_of(n * TILE, TILE), TILE)
        out = None
        for slot, j in ((0, 0), (1, 1), (10, 2), (11, 3)):
            lhs = arr[slot, :, :, :, at_n].reshape(16 * ROWS, TILE)
            rhs = og[j].reshape(16 * ROWS, D)
            product = lax.dot_general(lhs, rhs, TN, preferred_element_type=F32)
            out = product if out is None else out + product
        total[at_n, :] = out
        tile_copy(n).start()

    @pl.loop(0, F // TILE)
    def _(n):
        tile_copy(n).wait()

    for copy in copies:
        copy.wait()


def finish(*values):
    values = [pltpu.with_memory_space_constraint(v, pltpu.VMEM) for v in values]
    return pl.pallas_call(
        _finish,
        out_shape=[pltpu.HBM(v.shape, v.dtype) for v in values[:3]] + [pltpu.HBM((F, D), F32)],
        in_specs=[pl.BlockSpec(memory_space=pltpu.VMEM)] * 5,
        out_specs=[pl.BlockSpec(memory_space=pl.ANY)] * 4,
        scratch_shapes=[
            pltpu.VMEM((F, D), F32),
            pltpu.SemaphoreType.DMA((3, N)),
            pltpu.SemaphoreType.DMA((F // TILE,)),
        ],
        compiler_params=pltpu.CompilerParams(vmem_limit_bytes=12 << 20),
        name="finish",
    )(*values)


def body(inputs, out_grad, gate_pre, up_pre, gate_weight, up_weight, down_weight):
    values = exchange(out_grad, inputs, gate_pre, up_pre, gate_weight, up_weight, down_weight)
    return tuple(finish(*values))


def solution(mesh):
    in_specs = (
        P("col", "row"),
        P("col", "row"),
        P("row", "col"),
        P("row", "col"),
        P("row", "col"),
        P("row", "col"),
        P("col", "row"),
    )
    out_specs = (P("col", "row"), P("row", "col"), P("row", "col"), P("col", "row"))
    return jax.shard_map(body, mesh=mesh, in_specs=in_specs, out_specs=out_specs, check_vma=False)
```
